128 devices in a mesh: fsdp: 16 (over y, x_lo, core), ctx: 8 (over z, x_hi).
Axes of the slice: x: 4 (x_hi: 2, x_lo: 2; x = x_hi * 2 + x_lo), y: 4, z: 4, core: 2. Of those that a mesh axis runs over, the one named last changes fastest.
Arguments:
- tokens: bfloat16 [16384, 768], P(('fsdp', 'ctx')), may hold values from -24 to 24
- w_qkv: bfloat16 [768, 2304], P('fsdp'), may hold values from -0.21875 to 0.21875
- w_out: bfloat16 [768, 768], P('fsdp'), may hold values from -1.75 to 1.75
- w_up: bfloat16 [768, 3072], P('fsdp'), may hold values from -0.21875 to 0.21875
- w_down: bfloat16 [3072, 768], P('fsdp'), may hold values from -0.109375 to 0.109375
- vectors: bfloat16 [8, 768], P(None, 'fsdp'), may hold values from -0.9 to 1.75
- b_up: bfloat16 [3072], P('fsdp'), may hold values from -3 to 3
- lengths: int32 [16, 3], P('fsdp'), may hold values from 1 to 512, as said below
- block_seq: int32 [16, 8], P('fsdp'), may hold values from 0 to 2, as said below
- out_grad: bfloat16 [16384, 768], P(('fsdp', 'ctx')), may hold values from -6 to 6
Outputs:
- layer_out: bfloat16 [16384, 768], P(('fsdp', 'ctx'))
- tokens_grad: float32 [16384, 768], P(('fsdp', 'ctx'))
- qkv_grad: float32 [768, 2304], P('fsdp')
- out_proj_grad: float32 [768, 768], P('fsdp')
- up_grad: float32 [768, 3072], P('fsdp')
- down_grad: float32 [3072, 768], P('fsdp')
- vectors_grad: float32 [8, 768], P(None, 'fsdp')
- up_bias_grad: float32 [3072], P('fsdp')
The draws below stay inside these ranges and needn't reach their ends.
Inputs may be any that keep to these rules, and one draw needn't show every extreme that they name: In each group one sequence has exactly 512 tokens; sequence s of group g fills ceil(lengths[g, s] / 128) block slots. `block_seq`: every sequence of a group holds one block slot or more.
All inputs are finite; a program needn't handle non-finite values.
Results may differ from the reference program's by a relative error of at most 0.025.
Values may be sent and summed in bfloat16 or wider, within the bound.
No kernel may reach another device: no remote copies, remote signals or barrier semaphores. Data moves between devices by JAX's collectives and lax.ppermute only.
A program may use at most 128 MiB of HBM per device.

```python
from functools import partial
import jax
import jax.numpy as jnp
from jax import lax

D = 768
HEADS = 12
HD = 64
FF = 3072
BLK = 128
SPAN = 1024
NBLK = 8
SEQS = 3
TOKENS = 16384
N_FSDP = 16


def group_layout(key):
    key_extra, key_tail, key_order, key_label = jax.random.split(key, 4)
    long_blocks = NBLK // 2
    others = SEQS - 1
    extra_picks = jax.random.randint(key_extra, (long_blocks - others,), 0, others)
    other_counts = 1 + jnp.sum((extra_picks[:, None] == jnp.arange(others, dtype=jnp.int32)[None, :]).astype(jnp.int32), axis=0)
    counts = jnp.concatenate([jnp.full((1,), long_blocks, jnp.int32), other_counts.astype(jnp.int32)])
    tail_fill = jax.random.randint(key_tail, (SEQS,), 1, BLK + 1)
    raw_lengths = jnp.where(jnp.arange(SEQS, dtype=jnp.int32) == 0, long_blocks * BLK, (counts - 1) * BLK + tail_fill)
    block_ends = jnp.cumsum(counts)
    raw_ids = jnp.sum((jnp.arange(NBLK, dtype=jnp.int32)[:, None] >= block_ends[None, :]).astype(jnp.int32), axis=1)
    middle = jnp.concatenate([jnp.arange(1, NBLK // 2, dtype=jnp.int32), jnp.arange(NBLK // 2 + 1, NBLK - 1, dtype=jnp.int32)])
    slot_order = jnp.concatenate([jnp.array([0, NBLK - 1, NBLK // 2], jnp.int32), jax.random.permutation(key_order, middle)])
    raw_slots = jnp.zeros((NBLK,), jnp.int32).at[slot_order].set(raw_ids)
    labels = jax.random.permutation(key_label, SEQS).astype(jnp.int32)
    slot_ids = labels[raw_slots]
    seq_lengths = jnp.zeros((SEQS,), jnp.int32).at[labels].set(raw_lengths.astype(jnp.int32))
    return (seq_lengths, slot_ids)


def layouts(key):
    group_keys = jax.random.split(key, TOKENS // SPAN)
    return jax.vmap(group_layout)(group_keys)


def draw_lengths(key, part):
    shared = layouts(key)
    return shared[0]


def draw_block_seq(key, part):
    shared = layouts(key)
    return shared[1]


def draw_vectors(key, part):
    key = jax.random.fold_in(key, 3)
    spread_base = jnp.clip(jax.random.normal(key, (8, D), jnp.float32), -3.0, 3.0)
    row_scale = jnp.array([0.3, 0.05, 0.3, 0.3, 0.25, 0.3, 0.25, 0.3], jnp.float32)
    offset = jnp.array([0.0, 0.0, 0.0, 0.0, 1.0, 0.0, 1.0, 0.0], jnp.float32)
    return (offset[:, None] + row_scale[:, None] * spread_base).astype(jnp.bfloat16)


def spiked(entries, rng, source, target, parts, factor):
    owner, partner = [(jnp.arange(entries.shape[axis_at]) // (entries.shape[axis_at] // parts)).reshape([-1 if axis == axis_at else 1 for axis in range(entries.ndim)]) for axis_at in (source, target)]
    chosen = jax.random.permutation(rng, parts)[partner]
    strong = (owner == chosen) | (owner == (partner + parts // 2) % parts)
    return jnp.where(strong, factor * entries, entries)


def block_levels(own_key, shape, pieces, low, high):
    def one(axis_at, shards_of):
        heights = jax.random.uniform(jax.random.fold_in(jax.random.fold_in(own_key, 6), axis_at), (shards_of,), jnp.float32, low / len(pieces), high / len(pieces))
        return jnp.repeat(jnp.exp(heights), shape[axis_at] // shards_of).reshape((-1,) + (1,) * (len(shape) - axis_at - 1))

    gain = one(*pieces[0])
    for cut in pieces[1:]:
        gain = gain * one(*cut)
    return gain


def centred(stream_key, dims, scale, reach, pieces=(), kind=jnp.bfloat16):
    values = jax.random.normal(stream_key, dims, jnp.float32) * scale
    if len(pieces) > 0:
        values = block_levels(stream_key, dims, pieces, -0.22, 0.18) * values
    return jnp.clip(values, min=-reach, max=reach).astype(kind)


def noise_with(rng, dims, spread, reach, cuts, heavy, kind=jnp.bfloat16):
    values = spread * jax.random.normal(rng, dims, jnp.float32)
    if cuts:
        values = values * block_levels(rng, dims, cuts, -0.22, 0.18)
    return jnp.clip(spiked(values, jax.random.fold_in(rng, 3), *heavy), -reach, reach).astype(kind)


def setup_inputs(seed: int = 0) -> dict:
    seeds = jax.random.split(jax.random.key(seed), 11)
    tokens = noise_with(seeds[0], (TOKENS, D), 1.0, 24.0, ((0, 128),), (0, 1, 128, 5.5))
    w_qkv = centred(seeds[1], (D, 3 * D), D ** -0.5, 0.21875, ((0, 16),))
    w_out = centred(seeds[2], (D, D), (max(D // 64, 1)) ** -0.5, 1.75, ((0, 16),))
    w_up = centred(seeds[3], (D, FF), D ** -0.5, 0.21875, ((0, 16),))
    w_down = centred(seeds[4], (FF, D), FF ** -0.5, 0.109375, ((0, 16),))
    vectors = draw_vectors(jax.random.fold_in(seeds[10], 71), 0)
    b_up = centred(seeds[6], (FF,), 0.5, 3.0, ((0, 16),))
    lengths = draw_lengths(jax.random.fold_in(seeds[10], 71), 0)
    block_seq = draw_block_seq(jax.random.fold_in(seeds[10], 71), 0)
    out_grad = centred(seeds[9], (TOKENS, D), 1.0, 6.0, ((0, 128),))
    return dict(tokens=tokens, w_qkv=w_qkv, w_out=w_out, w_up=w_up, w_down=w_down, vectors=vectors, b_up=b_up, lengths=lengths, block_seq=block_seq, out_grad=out_grad)


epsilon = 1e-12
masked_fill = -1e+30
highest = lax.Precision.HIGHEST

@jax.custom_vjp
def low(v):
    return lax.optimization_barrier(v.astype(jnp.bfloat16)).astype(jnp.float32)

@jax.custom_vjp
def low_back(v):
    return v

def low_keep(v):
    return (low(v), None)

def low_pass(kept, grad):
    return (grad,)

def back_keep(v):
    return (v, None)

def back_low(kept, grad):
    return (low(grad),)
low.defvjp(low_keep, low_pass)
low_back.defvjp(back_keep, back_low)

def matmul_high(left_side, right_side):
    return jnp.dot(left_side, right_side, precision=highest)

def layer_norm(hidden, norm_gain, norm_shift):
    centre = hidden - lax.optimization_barrier(jnp.mean(hidden, axis=-1, keepdims=True))
    variance = lax.optimization_barrier(jnp.mean(centre * centre, axis=-1, keepdims=True))
    return centre * lax.rsqrt(variance + epsilon) * norm_gain + norm_shift

def slot_tables(length_row, seq_row):
    slot_index = jnp.arange(NBLK, dtype=jnp.int32)
    same_seq = seq_row[:, None] == seq_row[None, :]
    earlier = slot_index[None, :] < slot_index[:, None]
    block_rank = lax.optimization_barrier(jnp.sum((same_seq & earlier).astype(jnp.int32), axis=1))
    owner_len = lax.optimization_barrier(jnp.sum(jnp.where(seq_row[:, None] == jnp.arange(SEQS, dtype=jnp.int32)[None, :], length_row[None, :], 0), axis=1))
    block_fill = jnp.clip(owner_len - BLK * block_rank, 0, BLK)
    slot_seq = jnp.repeat(seq_row, BLK, total_repeat_length=SPAN)
    slot_fill = jnp.repeat(block_fill, BLK, total_repeat_length=SPAN)
    slot_valid = jnp.arange(SPAN, dtype=jnp.int32) % BLK < slot_fill
    return (slot_seq, slot_valid)

def group_forward(weights, inputs, slot_seq, slot_valid):
    w_qkv, w_out, w_up, w_down, vectors, b_up = weights
    score_scale = HD ** (-0.5)
    bias_qkv = jnp.concatenate([vectors[0], jnp.zeros_like(vectors[0]), vectors[1]])
    projected = low(low_back(matmul_high(inputs, w_qkv) + bias_qkv))
    query_heads = projected[:, :D].reshape(SPAN, HEADS, HD)
    key_heads = projected[:, D:2 * D].reshape(SPAN, HEADS, HD)
    value_heads = projected[:, 2 * D:].reshape(SPAN, HEADS, HD)
    key_mask = (slot_seq[:, None] == slot_seq[None, :]) & slot_valid[None, :]
    scores = jnp.einsum('qhd,khd->hqk', query_heads, key_heads, precision=highest) * score_scale
    scores = low_back(jnp.where(key_mask[None], scores, masked_fill))
    chances = jnp.exp(scores - jax.nn.logsumexp(scores, axis=-1, keepdims=True))
    mixture = jnp.einsum('hqk,khd->qhd', low(chances), value_heads, precision=highest).reshape(SPAN, D)
    mixture = low(low_back(mixture))
    attended = low_back(matmul_high(mixture, w_out) + vectors[2])
    first_norm = layer_norm(inputs + attended, vectors[4], vectors[5])
    up_proj = low_back(matmul_high(low(first_norm), w_up) + b_up)
    down_proj = low_back(matmul_high(low(jax.nn.gelu(up_proj, approximate=False)), w_down) + vectors[3])
    return layer_norm(first_norm + down_proj, vectors[6], vectors[7])

def reference(tokens, w_qkv, w_out, w_up, w_down, vectors, b_up, lengths, block_seq, out_grad):
    slot_seq, slot_valid = jax.vmap(slot_tables)(lengths, block_seq)
    inputs = tokens.astype(jnp.float32).reshape(N_FSDP, SPAN, D)
    weights = (w_qkv.astype(jnp.float32), w_out.astype(jnp.float32), w_up.astype(jnp.float32), w_down.astype(jnp.float32), vectors.astype(jnp.float32), b_up.astype(jnp.float32))

    def whole_layer(inputs, weights):
        group_step = jax.checkpoint(partial(group_forward, weights))
        return lax.map(lambda member: group_step(member[0], member[1], member[2]), (inputs, slot_seq, slot_valid))
    result, pull_back = jax.vjp(whole_layer, inputs, weights)
    input_grad, weight_grads = pull_back(out_grad.astype(jnp.float32).reshape(N_FSDP, SPAN, D))
    return (result.reshape(TOKENS, D).astype(jnp.bfloat16), input_grad.reshape(TOKENS, D), weight_grads[0], weight_grads[1], weight_grads[2], weight_grads[3], weight_grads[4], weight_grads[5])
```

```python
import jax
import jax.numpy as jnp
from jax import lax
from jax.experimental import pallas as pl
from jax.experimental.pallas import tpu as pltpu
from jax.sharding import PartitionSpec as P

D = 768
HD = 64
BLK = 128
NBLK = 8
SEQS = 3
SLOTS = 4
LOCAL = 3
WIDE = LOCAL * HD
FF = 3072
HALF = FF // 2
F = 16

epsilon = 1e-12
masked_fill = -1e30
root_half = 0.7071067811865476
inv_root_tau = 0.3989422804014327

bf16 = jnp.bfloat16
f32 = jnp.float32

VM = pl.BlockSpec(memory_space=pltpu.VMEM)
SM = pl.BlockSpec(memory_space=pltpu.SMEM)


def params():
    return pltpu.CompilerParams(vmem_limit_bytes=56 * 1024 * 1024)


def nn(a, b):
    return lax.dot_general(a, b, (((1,), (0,)), ((), ())), preferred_element_type=f32)


def nt(a, b):
    return lax.dot_general(a, b, (((1,), (1,)), ((), ())), preferred_element_type=f32)


def tn(a, b):
    return lax.dot_general(a, b, (((0,), (0,)), ((), ())), preferred_element_type=f32)


def call(kernel, name, out_shape, in_specs, scratch=(), flops=0, nbytes=0):
    return pl.pallas_call(
        kernel,
        out_shape=out_shape,
        in_specs=in_specs,
        out_specs=jax.tree.map(lambda _: VM, out_shape),
        scratch_shapes=list(scratch),
        compiler_params=params(),
        cost_estimate=pl.CostEstimate(flops=flops, bytes_accessed=nbytes, transcendentals=0),
        name=name,
    )


def shape(dims, dtype=f32):
    return jax.ShapeDtypeStruct(dims, dtype)


def slot_table(meta, table):
    xh = meta[0]
    for i in range(4):
        own = meta[4 + 2 * i + xh]
        for k in range(SLOTS):
            table[SLOTS * i + k] = 0
        count = jnp.int32(0)
        for b in range(NBLK):
            same = meta[4 + b] == own

            @pl.when(same)
            def _(i=i, b=b, count=count):
                table[SLOTS * i + jnp.minimum(count, SLOTS - 1)] = b

            count = count + same.astype(jnp.int32)


def attend_kernel(meta, x, w, bias, chances, query, keys, values, mixture, table):
    slot_table(meta, table)
    xh = meta[0]
    xs = x[...].reshape(NBLK * BLK, D)
    key_all = nn(xs, w[:, WIDE : 2 * WIDE]).astype(bf16)
    value_all = (nn(xs, w[:, 2 * WIDE : 3 * WIDE]) + bias[1:2, :]).astype(bf16)
    for h in range(LOCAL):
        keys[h] = key_all[:, HD * h : HD * h + HD]
        values[h] = value_all[:, HD * h : HD * h + HD]
    xq = jnp.concatenate([x[2 * i + xh] for i in range(4)], axis=0)
    q_all = (nn(xq, w[:, :WIDE]) + bias[0:1, :]).astype(bf16) * bf16(HD**-0.5)
    for h in range(LOCAL):
        query[h] = q_all[:, HD * h : HD * h + HD]
    lane = lax.broadcasted_iota(jnp.int32, (1, BLK), 1)
    for i in range(4):
        length = meta[1 + meta[4 + 2 * i + xh]]
        blank = jnp.concatenate(
            [jnp.where(lane < length - BLK * k, 0.0, masked_fill) for k in range(SLOTS)], axis=1
        )
        picks = [pl.ds(pl.multiple_of(table[SLOTS * i + k] * BLK, BLK), BLK) for k in range(SLOTS)]
        outs = []
        for h in range(LOCAL):
            key_h = jnp.concatenate([keys[h, p, :] for p in picks], axis=0)
            value_h = jnp.concatenate([values[h, p, :] for p in picks], axis=0)
            scores = nt(query[h, BLK * i : BLK * i + BLK, :], key_h) + blank
            peak = jnp.max(scores, axis=-1, keepdims=True)
            raised = jnp.exp(scores - peak)
            share = (raised * (1.0 / jnp.sum(raised, axis=-1, keepdims=True))).astype(bf16)
            chances[i, h] = share
            outs.append(nn(share, value_h))
        mixture[i] = jnp.concatenate(outs, axis=1).astype(bf16)


def attend(meta, x_all, w_heads, bias):
    return call(
        attend_kernel,
        "attend",
        (
            shape((4, LOCAL, BLK, SLOTS * BLK), bf16),
            shape((LOCAL, 4 * BLK, HD), bf16),
            shape((LOCAL, NBLK * BLK, HD), bf16),
            shape((LOCAL, NBLK * BLK, HD), bf16),
            shape((4, BLK, WIDE), bf16),
        ),
        [SM, VM, VM, VM],
        [pltpu.SMEM((4 * SLOTS,), jnp.int32)],
        flops=2 * 10**9,
        nbytes=6 * 10**6,
    )(meta, x_all, w_heads, bias)


def attend_back_kernel(
    meta, x, w, cot, chances, query, keys, values, grad_w, partial, sums, table, key_acc, value_acc
):
    slot_table(meta, table)
    xh = meta[0]
    key_acc[...] = jnp.zeros_like(key_acc)
    value_acc[...] = jnp.zeros_like(value_acc)
    query_cots = []
    for i in range(4):
        picks = [pl.ds(pl.multiple_of(table[SLOTS * i + k] * BLK, BLK), BLK) for k in range(SLOTS)]
        parts = []
        cot_i = cot[i]
        for h in range(LOCAL):
            key_h = jnp.concatenate([keys[h, p, :] for p in picks], axis=0)
            value_h = jnp.concatenate([values[h, p, :] for p in picks], axis=0)
            cot_h = cot_i[:, HD * h : HD * h + HD]
            share_low = chances[i, h]
            share = share_low.astype(f32)
            chance_cot = nt(cot_h, value_h)
            inner = jnp.sum(share * chance_cot, axis=-1, keepdims=True)
            score_cot = (share * (chance_cot - inner)).astype(bf16)
            parts.append(nn(score_cot, key_h))
            key_part = tn(score_cot, query[h, BLK * i : BLK * i + BLK, :])
            value_part = tn(share_low, cot_h)
            for k, p in enumerate(picks):
                key_acc[h, p, :] += key_part[BLK * k : BLK * k + BLK]
                value_acc[h, p, :] += value_part[BLK * k : BLK * k + BLK]
        query_cots.append((jnp.concatenate(parts, axis=1) * HD**-0.5).astype(bf16))
    query_cot = jnp.concatenate(query_cots, axis=0)
    key_cot = jnp.concatenate([key_acc[h] for h in range(LOCAL)], axis=1).astype(bf16)
    value_cot = jnp.concatenate([value_acc[h] for h in range(LOCAL)], axis=1).astype(bf16)
    xs = x[...].reshape(NBLK * BLK, D)
    xq = jnp.concatenate([x[2 * i + xh] for i in range(4)], axis=0)
    grad_w[:, :WIDE] = tn(xq, query_cot).astype(bf16)
    grad_w[:, WIDE : 2 * WIDE] = tn(xs, key_cot).astype(bf16)
    grad_w[:, 2 * WIDE : 3 * WIDE] = tn(xs, value_cot).astype(bf16)
    sums[0:1] = jnp.sum(query_cot.astype(f32), axis=0, keepdims=True)
    sums[1:2] = jnp.sum(value_cot.astype(f32), axis=0, keepdims=True)
    key_value = nt(key_cot, w[:, WIDE : 2 * WIDE]) + nt(value_cot, w[:, 2 * WIDE : 3 * WIDE])
    query_part = nt(query_cot, w[:, :WIDE])
    for i in range(4):
        row = BLK * 2 * i
        both = [key_value[row : row + BLK], key_value[row + BLK : row + 2 * BLK]]
        mine = query_part[BLK * i : BLK * i + BLK]
        partial[2 * i] = (both[0] + jnp.where(xh == 0, mine, 0.0)).astype(bf16)
        partial[2 * i + 1] = (both[1] + jnp.where(xh == 1, mine, 0.0)).astype(bf16)


def attend_back(meta, x_all, w_heads, cot, kept):
    return call(
        attend_back_kernel,
        "attend_back",
        (shape((D, LOCAL * WIDE), bf16), shape((NBLK, BLK, D), bf16), shape((2, WIDE))),
        [SM] + [VM] * 7,
        [
            pltpu.SMEM((4 * SLOTS,), jnp.int32),
            pltpu.VMEM((LOCAL, NBLK * BLK, HD), f32),
            pltpu.VMEM((LOCAL, NBLK * BLK, HD), f32),
        ],
        flops=5 * 10**9,
        nbytes=10**7,
    )(meta, x_all, w_heads, cot, *kept)


def centred(hidden):
    centre = hidden - jnp.mean(hidden, axis=-1, keepdims=True)
    inverse = lax.rsqrt(jnp.mean(centre * centre, axis=-1, keepdims=True) + epsilon)
    return centre * inverse, inverse


def norm_back(scaled, hat, inverse):
    return inverse * (
        scaled
        - jnp.mean(scaled, axis=-1, keepdims=True)
        - hat * jnp.mean(scaled * hat, axis=-1, keepdims=True)
    )


def first_kernel(mixture, weights, vectors, tokens, norm, low, hat, inverse):
    w_out = weights[:, 192:240, :].reshape(D, D)
    total = nn(mixture[0], w_out[:WIDE])
    for z in range(1, 4):
        total += nn(mixture[z], w_out[WIDE * z : WIDE * z + WIDE])
    first_hat, first_inv = centred(tokens[...].astype(f32) + (total + vectors[2:3]))
    first_norm = first_hat * vectors[4:5] + vectors[5:6]
    norm[...] = first_norm
    low[...] = first_norm.astype(bf16)
    hat[...] = first_hat
    inverse[...] = first_inv


def feed_kernel(mine, other, weights, b_up, activ, slope, keep, send):
    rows = jnp.concatenate([mine[...], other[...]], axis=0)
    total = None
    for j in range(2):
        w_up = weights[:, 96 + 48 * j : 144 + 48 * j, :].reshape(D, D)
        up = nn(rows, w_up) + b_up[:, D * j : D * j + D]
        erf = lax.erf(up * root_half)
        low = (0.5 * up * (1.0 + erf)).astype(bf16)
        activ[:, D * j : D * j + D] = low
        slope[:, D * j : D * j + D] = (
            0.5 * (1.0 + erf) + up * jnp.exp(-0.5 * up * up) * inv_root_tau
        ).astype(bf16)
        w_down = weights[8 * j : 8 * j + 8, 0:96, :].reshape(D, D)
        part = nn(low, w_down)
        total = part if total is None else total + part
    keep[...] = total[:BLK]
    send[...] = total[BLK:].astype(bf16)


def second_kernel(norm, keep, came, vectors, out_grad, layer_out, cot, low, sums):
    second_sum = norm[...] + (keep[...] + came[...].astype(f32)) + vectors[3:4]
    second_hat, second_inv = centred(second_sum)
    layer_out[...] = (second_hat * vectors[6:7] + vectors[7:8]).astype(bf16)
    out_cot = out_grad[...].astype(f32)
    second_cot = norm_back(out_cot * vectors[6:7], second_hat, second_inv)
    cot[...] = second_cot
    down_cot = second_cot.astype(bf16)
    low[...] = down_cot
    sums[0:1] = jnp.sum(down_cot.astype(f32), axis=0, keepdims=True)
    sums[1:2] = jnp.sum(out_cot * second_hat, axis=0, keepdims=True)
    sums[2:3] = jnp.sum(out_cot, axis=0, keepdims=True)


def feed_back_kernel(mine, other, weights, slope, up_cot, keep, send, sums):
    rows = jnp.concatenate([mine[...], other[...]], axis=0)
    total = None
    for j in range(2):
        w_down = weights[8 * j : 8 * j + 8, 0:96, :].reshape(D, D)
        w_up = weights[:, 96 + 48 * j : 144 + 48 * j, :].reshape(D, D)
        low = (nt(rows, w_down) * slope[:, D * j : D * j + D].astype(f32)).astype(bf16)
        up_cot[:, D * j : D * j + D] = low
        sums[:, D * j : D * j + D] = jnp.sum(low.astype(f32), axis=0, keepdims=True)
        part = nt(low, w_up)
        total = part if total is None else total + part
    keep[...] = total[:BLK]
    send[...] = total[BLK:].astype(bf16)


def feed_grad_kernel(mine, other, low_mine, low_other, activ, up_cot, grads):
    down_cot = jnp.concatenate([mine[...], other[...]], axis=0)
    first_low = jnp.concatenate([low_mine[...], low_other[...]], axis=0)
    for j in range(2):
        down = tn(activ[:, D * j : D * j + D], down_cot).astype(bf16)
        grads[8 * j : 8 * j + 8, 0:96, :] = down.reshape(8, 96, D)
        up = tn(first_low, up_cot[:, D * j : D * j + D]).astype(bf16)
        grads[:, 96 + 48 * j : 144 + 48 * j, :] = up.reshape(F, 48, D)


def first_back_kernel(
    cot, keep, came, vectors, hat, inverse, weights, mixture, input_cot, back, grad_out, sums
):
    first_cot = cot[...] + (keep[...] + came[...].astype(f32))
    first_hat = hat[...]
    total = norm_back(first_cot * vectors[4:5], first_hat, inverse[...])
    input_cot[...] = total
    attend_cot = total.astype(bf16)
    sums[0:1] = jnp.sum(attend_cot.astype(f32), axis=0, keepdims=True)
    sums[1:2] = jnp.sum(first_cot * first_hat, axis=0, keepdims=True)
    sums[2:3] = jnp.sum(first_cot, axis=0, keepdims=True)
    w_out = weights[:, 192:240, :].reshape(D, D)
    for z in range(4):
        back[z] = nt(attend_cot, w_out[WIDE * z : WIDE * z + WIDE]).astype(bf16)
        grad_out[4 * z : 4 * z + 4] = (
            tn(mixture[z], attend_cot).astype(bf16).reshape(4, 48, D)
        )


CHIPS = [[i for i in range(F) if i % 2 == k] for k in range(2)]
ZS = [[0, 2, 4, 6], [1, 3, 5, 7]]
HALVES = [[0, 1, 4, 5], [2, 3, 6, 7]]


def swap(x, axis, size, bit):
    return lax.ppermute(x, axis, [(i, i ^ bit) for i in range(size)])


def a2a(x, axis, groups=None):
    return lax.all_to_all(x, axis, 0, 0, tiled=True, axis_index_groups=groups)


def spread(x, axis, n, groups=None):
    return a2a(jnp.broadcast_to(x[None], (n,) + x.shape), axis, groups)


def body(tokens, w_qkv, w_out, w_up, w_down, vectors, b_up, lengths, block_seq, out_grad):
    place = lax.axis_index("ctx")
    z, xh, half = place // 2, place % 2, (place // 2) % 2
    core = lax.axis_index("fsdp") % 2

    def pick(x, index, axis):
        return lax.dynamic_index_in_dim(x, index, axis, keepdims=False)

    feed_own = jnp.concatenate(
        [
            pick(w_down.reshape(2, 96, D), half, 0),
            pick(w_up.reshape(48, F, 2, 96), half, 2).reshape(48, 2, D).transpose(1, 0, 2).reshape(96, D),
            w_out,
        ],
        axis=0,
    )
    feed_w = lax.all_gather(feed_own, "fsdp", axis=0, tiled=False)
    heads_own = jnp.concatenate(
        [
            pick(w_qkv.reshape(48, 3, 4, WIDE), z, 2).reshape(48, 3 * WIDE),
            vectors.T,
            b_up.reshape(48, 4),
            jnp.zeros((48, 180), bf16),
        ],
        axis=1,
    )
    heads_mine = spread(heads_own, "fsdp", 8, CHIPS)
    heads_other = swap(heads_mine, "fsdp", F, 1)
    heads_w = jnp.where(
        core == 0,
        jnp.concatenate([heads_mine, heads_other], axis=1),
        jnp.concatenate([heads_other, heads_mine], axis=1),
    ).reshape(D, D)
    x_all = spread(tokens, "ctx", NBLK)

    rows = heads_w[:, 576:584].T.astype(f32)
    up_bias = pick(heads_w[:, 584:588].reshape(F, 2, 96), half, 1).reshape(1, HALF).astype(f32)
    head_bias = pick(rows[0:2].reshape(2, 4, WIDE), z, 1)
    meta = jnp.concatenate([xh[None], lengths[0], block_seq[0]]).astype(jnp.int32)

    *kept, mixture_part = attend(meta, x_all, heads_w, head_bias)
    mixture = a2a(mixture_part, "ctx", ZS)
    first_norm, first_low, first_hat, first_inv = call(
        first_kernel,
        "first",
        (shape((BLK, D)), shape((BLK, D), bf16), shape((BLK, D)), shape((BLK, 1))),
        [VM] * 4,
        flops=2 * BLK * D * D,
        nbytes=8 * 10**6,
    )(mixture, feed_w, rows, tokens)
    low_other = swap(first_low, "ctx", NBLK, 2)
    activ, slope, keep, send = call(
        feed_kernel,
        "feed",
        (shape((2 * BLK, HALF), bf16), shape((2 * BLK, HALF), bf16), shape((BLK, D)), shape((BLK, D), bf16)),
        [VM] * 4,
        flops=8 * BLK * D * HALF,
        nbytes=8 * 10**6,
    )(first_low, low_other, feed_w, up_bias)
    came = swap(send, "ctx", NBLK, 2)
    layer_out, second_cot, down_cot, second_sums = call(
        second_kernel,
        "second",
        (shape((BLK, D), bf16), shape((BLK, D)), shape((BLK, D), bf16), shape((3, D))),
        [VM] * 5,
        flops=10**7,
        nbytes=2 * 10**6,
    )(first_norm, keep, came, rows, out_grad)
    down_other = swap(down_cot, "ctx", NBLK, 2)
    up_cot, keep, send, up_sums = call(
        feed_back_kernel,
        "feed_back",
        (shape((2 * BLK, HALF), bf16), shape((BLK, D)), shape((BLK, D), bf16), shape((1, HALF))),
        [VM] * 4,
        flops=8 * BLK * D * HALF,
        nbytes=8 * 10**6,
    )(down_cot, down_other, feed_w, slope)
    came = swap(send, "ctx", NBLK, 2)
    feed_grads = call(
        feed_grad_kernel,
        "feed_grad",
        shape((F, 192, D), bf16),
        [VM] * 6,
        flops=8 * BLK * D * HALF,
        nbytes=8 * 10**6,
    )(down_cot, down_other, first_low, low_other, activ, up_cot)
    input_cot, back, out_grads, first_sums = call(
        first_back_kernel,
        "first_back",
        (shape((BLK, D)), shape((4, BLK, WIDE), bf16), shape((F, 48, D), bf16), shape((3, D))),
        [VM] * 8,
        flops=4 * BLK * D * D,
        nbytes=8 * 10**6,
    )(second_cot, keep, came, rows, first_hat, first_inv, feed_w, mixture)
    grads = jnp.concatenate([feed_grads, out_grads], axis=1)
    feed_sum = lax.psum_scatter(grads.reshape(F * 240, D), "fsdp", scatter_dimension=0, tiled=True)
    cot = a2a(back, "ctx", ZS)
    head_grads, partial, head_sums = attend_back(meta, x_all, heads_w, cot, kept)

    tokens_grad = input_cot + jnp.sum(a2a(partial, "ctx").astype(f32), axis=0)

    slot = (lax.broadcasted_iota(jnp.int32, (1, D), 1) // WIDE) == z
    head_rows = jnp.where(slot, jnp.tile(head_sums, (1, 4)), 0.0)
    vector_part = jnp.concatenate([head_rows, first_sums[0:1], second_sums[0:1], first_sums[1:3], second_sums[1:3]])
    extras = jnp.concatenate([vector_part.T, up_sums.reshape(D, 2), jnp.zeros((D, 182), f32)], axis=1)
    heads_grad = jnp.concatenate([head_grads, extras.astype(bf16)], axis=1).reshape(8, 2, 48, D)
    mine = pick(heads_grad, core, 1)
    other = swap(pick(heads_grad, 1 - core, 1), "fsdp", F, 1)
    pair = (mine.astype(f32) + other.astype(f32)).astype(bf16)
    heads_sum = jnp.sum(a2a(pair, "fsdp", CHIPS).astype(f32), axis=0).astype(bf16)

    padded = jnp.concatenate([feed_sum, jnp.zeros((16, D), bf16)], axis=0)
    quarter = jnp.sum(a2a(padded.reshape(4, 64, D), "ctx", HALVES).astype(f32), axis=0).astype(bf16)
    every = spread(jnp.concatenate([quarter, heads_sum], axis=0), "ctx", NBLK).astype(f32)

    halves = every[:, :64].reshape(2, 2, 2, 64, D).transpose(1, 0, 2, 3, 4).reshape(2, 256, D)
    down_grad = halves[:, :96].reshape(192, D)
    up_grad = jnp.stack(
        [jnp.concatenate([halves[h, 96:144], halves[h, 144:192]], axis=1).reshape(48, F, 96) for h in range(2)],
        axis=2,
    ).reshape(48, FF)
    out_proj_grad = halves[0, 192:240] + halves[1, 192:240]
    heads = every[:, 64:].reshape(4, 2, 48, 4, WIDE)
    by_z = heads[:, 0] + heads[:, 1]
    qkv_grad = by_z[:, :, :3].transpose(1, 2, 0, 3).reshape(48, 3 * D)
    extra = every[:, 64:, 576:586]
    vectors_grad = jnp.sum(extra[:, :, :8], axis=0).T
    ups = extra[:, :, 8:].reshape(2, 2, 2, 48, 2)
    up_bias_grad = jnp.sum(ups, axis=(0, 2)).reshape(192)
    return (layer_out, tokens_grad, qkv_grad, out_proj_grad, up_grad, down_grad, vectors_grad, up_bias_grad)


def solution(mesh):
    by_token = P(("fsdp", "ctx"), None)
    by_row = P("fsdp", None)
    in_specs = (
        by_token, by_row, by_row, by_row, by_row, P(None, "fsdp"), P("fsdp"), by_row, by_row, by_token,
    )
    out_specs = (by_token, by_token, by_row, by_row, by_row, by_row, P(None, "fsdp"), P("fsdp"))
    return jax.shard_map(body, mesh=mesh, in_specs=in_specs, out_specs=out_specs, check_vma=False)
```

```python
import jax
import jax.numpy as jnp
from jax import lax
from jax.experimental import pallas as pl
from jax.experimental.pallas import tpu as pltpu
from jax.sharding import PartitionSpec as P

D = 768
HD = 64
BLK = 128
NBLK = 8
SEQS = 3
SLOTS = 4
LOCAL = 3
WIDE = LOCAL * HD
FF = 3072
HALF = FF // 2
F = 16

epsilon = 1e-12
masked_fill = -1e30
root_half = 0.7071067811865476
inv_root_tau = 0.3989422804014327

bf16 = jnp.bfloat16
f32 = jnp.float32

VM = pl.BlockSpec(memory_space=pltpu.VMEM)
SM = pl.BlockSpec(memory_space=pltpu.SMEM)
HB = pl.BlockSpec(memory_space=pltpu.HBM)
EXTRA = 640


def params(mib):
    return pltpu.CompilerParams(vmem_limit_bytes=mib * 1024 * 1024)


def nn(a, b):
    return lax.dot_general(a, b, (((1,), (0,)), ((), ())), preferred_element_type=f32)


def nt(a, b):
    return lax.dot_general(a, b, (((1,), (1,)), ((), ())), preferred_element_type=f32)


def tn(a, b):
    return lax.dot_general(a, b, (((0,), (0,)), ((), ())), preferred_element_type=f32)


def call(kernel, name, out_shape, in_specs, scratch=(), flops=0, nbytes=0, out_specs=None, mib=16):
    return pl.pallas_call(
        kernel,
        out_shape=out_shape,
        in_specs=in_specs,
        out_specs=jax.tree.map(lambda _: VM, out_shape) if out_specs is None else out_specs,
        scratch_shapes=list(scratch),
        compiler_params=params(mib),
        cost_estimate=pl.CostEstimate(flops=flops, bytes_accessed=nbytes, transcendentals=0),
        name=name,
    )


def shape(dims, dtype=f32):
    return jax.ShapeDtypeStruct(dims, dtype)


def places():
    place = lax.axis_index("ctx")
    return lax.rem(place, 2), lax.div(place, 2), lax.rem(lax.axis_index("fsdp"), 2)


def begin(sems, first, *pairs):
    copies = [pltpu.make_async_copy(a, b, sems.at[first + k]) for k, (a, b) in enumerate(pairs)]
    for copy in copies:
        copy.start()
    return copies


def finish(copies):
    for copy in copies:
        copy.wait()


def dma(n):
    return pltpu.SemaphoreType.DMA((n,))


def head_rows(w_mine, w_other, weights, row):
    core = places()[2]
    return (
        (w_mine.at[:, pl.ds(row, 48)], weights.at[:, core]),
        (w_other.at[:, pl.ds(row, 48)], weights.at[:, 1 - core]),
    )


def token_rows(tokens, other, pairs, x):
    xh, zed, _ = places()
    moves = [(tokens, x.at[2 * zed + xh]), (other, x.at[2 * zed + 1 - xh])]
    for k, pair in enumerate(pairs):
        z = zed ^ (k + 1)
        moves += [(pair.at[0], x.at[2 * z + xh]), (pair.at[1], x.at[2 * z + 1 - xh])]
    return moves


def slot_table(block_seq, table):
    xh, _, _ = places()
    for i in range(4):
        own = block_seq[0, 2 * i + xh]
        for k in range(SLOTS):
            table[SLOTS * i + k] = 0
        count = jnp.int32(0)
        for b in range(NBLK):
            same = block_seq[0, b] == own

            @pl.when(same)
            def _(i=i, b=b, count=count):
                table[SLOTS * i + jnp.minimum(count, SLOTS - 1)] = b

            count = count + same.astype(jnp.int32)


def attend_kernel(lengths, block_seq, tokens, other, pair1, pair2, pair3, w_mine, w_other, rows, *refs):
    kept_out, sends, refs = refs[:4], refs[4:8], refs[8:]
    x, own, weights, chances, query, keys, values, mixture, table, sems = refs
    loads = begin(sems, 0, *token_rows(tokens, other, (pair1, pair2, pair3), x))
    loads += begin(sems, 13, (tokens, own.at[places()[1]]))
    loads += begin(
        sems, 14, *((pair.at[0], own.at[places()[1] ^ (k + 1)]) for k, pair in enumerate((pair1, pair2, pair3)))
    )
    loads += begin(sems, 8, *head_rows(w_mine, w_other, weights, 0))
    slot_table(block_seq, table)
    xh, zed, core = places()
    finish(loads)
    w = weights[...].reshape(D, D)
    rows[...] = jnp.transpose(w[:, EXTRA:].astype(f32))[:16]
    bias = jnp.zeros((2, WIDE), f32)
    for z in range(4):
        bias = jnp.where(zed == z, rows[0:2, WIDE * z : WIDE * z + WIDE], bias)
    xs = x[...].reshape(NBLK * BLK, D)
    key_all = nn(xs, w[:, WIDE : 2 * WIDE]).astype(bf16)
    value_all = (nn(xs, w[:, 2 * WIDE : 3 * WIDE]) + bias[1:2, :]).astype(bf16)
    for h in range(LOCAL):
        keys[h] = key_all[:, HD * h : HD * h + HD]
        values[h] = value_all[:, HD * h : HD * h + HD]
    q_all = (nn(own[...].reshape(4 * BLK, D), w[:, :WIDE]) + bias[0:1, :]).astype(bf16) * bf16(HD**-0.5)
    for h in range(LOCAL):
        query[h] = q_all[:, HD * h : HD * h + HD]
    stores = begin(sems, 10, *zip((query, keys, values), kept_out[1:]))
    lane = lax.broadcasted_iota(jnp.int32, (1, BLK), 1)
    for i in range(4):
        length = lengths[0, block_seq[0, 2 * i + xh]]
        blank = jnp.concatenate(
            [jnp.where(lane < length - BLK * k, 0.0, masked_fill) for k in range(SLOTS)], axis=1
        )
        picks = [pl.ds(pl.multiple_of(table[SLOTS * i + k] * BLK, BLK), BLK) for k in range(SLOTS)]
        outs = []
        for h in range(LOCAL):
            key_h = jnp.concatenate([keys[h, p, :] for p in picks], axis=0)
            value_h = jnp.concatenate([values[h, p, :] for p in picks], axis=0)
            scores = nt(query[h, BLK * i : BLK * i + BLK, :], key_h) + blank
            peak = jnp.max(scores, axis=-1, keepdims=True)
            raised = jnp.exp(scores - peak)
            share = (raised * (1.0 / jnp.sum(raised, axis=-1, keepdims=True))).astype(bf16)
            chances[i, h] = share
            outs.append(nn(share, value_h))
        mixture[zed ^ i] = jnp.concatenate(outs, axis=1).astype(bf16)
    stores += begin(sems, 0, *((mixture.at[k], out) for k, out in enumerate(sends)), (chances, kept_out[0]))
    finish(stores)


KEPT = (
    shape((4, LOCAL, BLK, SLOTS * BLK), bf16),
    shape((LOCAL, 4 * BLK, HD), bf16),
    shape((LOCAL, NBLK * BLK, HD), bf16),
    shape((LOCAL, NBLK * BLK, HD), bf16),
)
KEPT_VMEM = [pltpu.VMEM(one.shape, one.dtype) for one in KEPT]


def attend(lengths, block_seq, blocks, w_mine, w_other):
    return call(
        attend_kernel,
        "attend",
        (shape((16, D)),) + KEPT + (shape((BLK, WIDE), bf16),) * 4,
        [SM, SM] + [HB] * 7,
        [pltpu.VMEM((NBLK, BLK, D), bf16), pltpu.VMEM((4, BLK, D), bf16), pltpu.VMEM((8, 2, 48, D), bf16)]
        + KEPT_VMEM
        + [pltpu.VMEM((4, BLK, WIDE), bf16), pltpu.SMEM((4 * SLOTS,), jnp.int32), dma(17)],
        mib=56,
        flops=2 * 10**9,
        nbytes=6 * 10**6,
        out_specs=(VM,) + (HB,) * 8,
    )(lengths, block_seq, *blocks, w_mine, w_other)


def attend_back_kernel(block_seq, w_mine, w_other, *refs):
    cots, kept, refs = refs[:4], refs[4:8], refs[8:]
    query_out, key_out, value_out, part0, part1, part2, part3, weights, chances, query, keys, values = refs[:12]
    table, key_acc, value_acc, cot, partial, sems = refs[12:]
    xh, zed, core = places()
    loads = begin(sems, 0, *((one, cot.at[zed ^ k]) for k, one in enumerate(cots)))
    loads += begin(sems, 4, *zip(kept, (chances, query, keys, values)))
    late = begin(sems, 8, *head_rows(w_mine, w_other, weights, 0))
    slot_table(block_seq, table)
    key_acc[...] = jnp.zeros_like(key_acc)
    value_acc[...] = jnp.zeros_like(value_acc)
    finish(loads)
    query_cots = []
    for i in range(4):
        picks = [pl.ds(pl.multiple_of(table[SLOTS * i + k] * BLK, BLK), BLK) for k in range(SLOTS)]
        parts = []
        cot_i = cot[i]
        for h in range(LOCAL):
            key_h = jnp.concatenate([keys[h, p, :] for p in picks], axis=0)
            value_h = jnp.concatenate([values[h, p, :] for p in picks], axis=0)
            cot_h = cot_i[:, HD * h : HD * h + HD]
            share_low = chances[i, h]
            share = share_low.astype(f32)
            chance_cot = nt(cot_h, value_h)
            inner = jnp.sum(share * chance_cot, axis=-1, keepdims=True)
            score_cot = (share * (chance_cot - inner)).astype(bf16)
            parts.append(nn(score_cot, key_h))
            key_part = tn(score_cot, query[h, BLK * i : BLK * i + BLK, :])
            value_part = tn(share_low, cot_h)
            for k, p in enumerate(picks):
                key_acc[h, p, :] += key_part[BLK * k : BLK * k + BLK]
                value_acc[h, p, :] += value_part[BLK * k : BLK * k + BLK]
        query_cots.append((jnp.concatenate(parts, axis=1) * HD**-0.5).astype(bf16))
    query_cot = jnp.concatenate(query_cots, axis=0)
    key_cot = jnp.concatenate([key_acc[h] for h in range(LOCAL)], axis=1).astype(bf16)
    value_cot = jnp.concatenate([value_acc[h] for h in range(LOCAL)], axis=1).astype(bf16)
    query_out[...] = query_cot
    key_out[...] = key_cot
    value_out[...] = value_cot
    finish(late)
    w = weights[...].reshape(D, D)
    key_value = nt(key_cot, w[:, WIDE : 2 * WIDE]) + nt(value_cot, w[:, 2 * WIDE : 3 * WIDE])
    query_part = nt(query_cot, w[:, :WIDE])
    for i in range(4):
        row = BLK * 2 * i
        mine_q = query_part[BLK * i : BLK * i + BLK]
        partial[zed ^ i, 0] = (
            jnp.where(xh == 0, key_value[row : row + BLK], key_value[row + BLK : row + 2 * BLK]) + mine_q
        ).astype(bf16)
        partial[zed ^ i, 1] = jnp.where(
            xh == 0, key_value[row + BLK : row + 2 * BLK], key_value[row : row + BLK]
        ).astype(bf16)
    stores = begin(sems, 0, *((partial.at[k], out) for k, out in enumerate((part0, part1, part2, part3))))
    finish(stores)


def attend_back(block_seq, w_mine, w_other, cots, kept):
    return call(
        attend_back_kernel,
        "attend_back",
        (shape((4 * BLK, WIDE), bf16), shape((NBLK * BLK, WIDE), bf16), shape((NBLK * BLK, WIDE), bf16))
        + (shape((2, BLK, D), bf16),) * 4,
        [SM] + [HB] * 10,
        [pltpu.VMEM((8, 2, 48, D), bf16)]
        + KEPT_VMEM
        + [
            pltpu.SMEM((4 * SLOTS,), jnp.int32),
            pltpu.VMEM((LOCAL, NBLK * BLK, HD), f32),
            pltpu.VMEM((LOCAL, NBLK * BLK, HD), f32),
            pltpu.VMEM((4, BLK, WIDE), bf16),
            pltpu.VMEM((4, 2, BLK, D), bf16),
            dma(10),
        ],
        mib=56,
        flops=4 * 10**9,
        nbytes=8 * 10**6,
        out_specs=(VM,) * 3 + (HB,) * 4,
    )(block_seq, w_mine, w_other, *cots, *kept)


def head_grad_kernel(
    tokens, other, pair1, pair2, pair3, query, keys, values, first_sums, second_sums, up_sums,
    mine, send, x, packed, sems,
):
    loads = begin(sems, 0, *token_rows(tokens, other, (pair1, pair2, pair3), x))
    xh, zed, core = places()
    query_cot, key_cot, value_cot = query[...], keys[...], values[...]
    finish(loads)
    xs = x[...].reshape(NBLK * BLK, D)
    xq = jnp.concatenate([x[2 * i + xh] for i in range(4)], axis=0)
    grads = jnp.concatenate(
        [tn(xq, query_cot), tn(xs, key_cot), tn(xs, value_cot), jnp.zeros((D, EXTRA - 3 * WIDE), f32)], axis=1
    ).astype(bf16)
    lane = lax.broadcasted_iota(jnp.int32, (2, D), 1)
    edge = zed * WIDE
    inside = (lane >= edge) & (lane < edge + WIDE)
    own = jnp.concatenate(
        [
            jnp.sum(query_cot.astype(f32), axis=0, keepdims=True),
            jnp.sum(value_cot.astype(f32), axis=0, keepdims=True),
        ],
        axis=0,
    )
    own = jnp.where(inside, jnp.concatenate([own] * 4, axis=1), 0.0)
    vec = jnp.concatenate(
        [first_sums[0:1], second_sums[0:1], first_sums[1:3], second_sums[1:3], up_sums[...]], axis=0
    )
    extra = jnp.concatenate([own, vec, jnp.zeros((118, D), f32)], axis=0)
    extra = jnp.transpose(extra).astype(bf16)
    for f in range(F):
        slot = core if f % 2 == 0 else 1 - core
        packed[slot, f // 2, :, :EXTRA] = grads[48 * f : 48 * f + 48]
        packed[slot, f // 2, :, EXTRA:] = extra[48 * f : 48 * f + 48]
    stores = begin(sems, 0, (packed.at[1], send), (packed.at[0], mine))
    finish(stores)


def head_grad(blocks, cots, sums):
    half = shape((8, 48, D), bf16)
    return call(
        head_grad_kernel,
        "head_grad",
        (half, half),
        [HB] * 5 + [VM] * 6,
        [pltpu.VMEM((NBLK, BLK, D), bf16), pltpu.VMEM((2, 8, 48, D), bf16), dma(8)],
        mib=56,
        flops=2 * 10**9,
        nbytes=4 * 10**6,
        out_specs=(HB, HB),
    )(*blocks, *cots, *sums)


def centred(hidden):
    centre = hidden - jnp.mean(hidden, axis=-1, keepdims=True)
    inverse = lax.rsqrt(jnp.mean(centre * centre, axis=-1, keepdims=True) + epsilon)
    return centre * inverse, inverse


def norm_back(scaled, hat, inverse):
    return inverse * (
        scaled
        - jnp.mean(scaled, axis=-1, keepdims=True)
        - hat * jnp.mean(scaled * hat, axis=-1, keepdims=True)
    )


def pack_kernel(vectors, b_up, w_qkv, w_out, w_up, w_down, heads, feed, heads_own, feed_own, qkv, up, sems):
    xh, zed, core = places()
    half = lax.rem(zed, 2)
    start = pl.multiple_of(96 * half, 32)
    loads = begin(
        sems,
        0,
        (w_qkv, qkv),
        (w_up, up),
        (w_out, heads_own.at[pl.ds(48, 48)]),
        (w_down.at[pl.ds(start, 96)], feed_own.at[pl.ds(0, 96)]),
    )
    bias = b_up[...].astype(f32)
    small = jnp.concatenate([vectors[...].astype(f32)] + [bias[:, 48 * e : 48 * e + 48] for e in range(4)], axis=0)
    small = jnp.concatenate([small, jnp.zeros((12, 80), f32)], axis=1)
    small = jnp.concatenate([small, jnp.zeros((116, 128), f32)], axis=0)
    heads_own[0:48, EXTRA:] = jnp.transpose(small)[:48].astype(bf16)
    heads_own[0:48, 3 * WIDE : EXTRA] = jnp.zeros((48, EXTRA - 3 * WIDE), bf16)
    loads[0].wait()
    for z in range(4):

        @pl.when(zed == z)
        def _(z=z):
            heads_own[0:48, : 3 * WIDE] = jnp.concatenate(
                [qkv[:, D * t + WIDE * z : D * t + WIDE * z + WIDE] for t in range(3)], axis=1
            )

    loads[2].wait()
    stores = begin(sems, 4, *((heads_own, heads.at[k]) for k in range(8)))
    loads[1].wait()
    for h in range(2):

        @pl.when(half == h)
        def _(h=h):
            for e in range(2):
                first = 96 * h + 48 * e
                feed_own[96 + 48 * e : 144 + 48 * e, :] = jnp.concatenate(
                    [up[:, 192 * f + first : 192 * f + first + 48] for f in range(F)], axis=1
                )

    loads[3].wait()
    stores += begin(sems, 12, *((feed_own, feed.at[k]) for k in range(8)))
    finish(stores)


def first_kernel(mix0, mix1, mix2, mix3, w_mine, w_other, vectors, tokens, low, norm, hat, *scratch):
    weights, mixes, norm_own, hat_own, sems = scratch
    xh, zed, core = places()
    loads = begin(sems, 0, *((mix, mixes.at[k]) for k, mix in enumerate((mix0, mix1, mix2, mix3))))
    loads += begin(sems, 4, *head_rows(w_mine, w_other, weights, 48))
    total = tokens[...].astype(f32) + vectors[2:3]
    finish(loads)
    for k in range(4):
        total += nn(mixes[k], weights[pl.ds(2 * (zed ^ k), 2)].reshape(WIDE, D))
    first_hat, first_inv = centred(total)
    first_norm = first_hat * vectors[4:5] + vectors[5:6]
    low[...] = first_norm.astype(bf16)
    norm_own[...] = first_norm
    hat_own[:, :D] = first_hat
    hat_own[:, D:] = jnp.broadcast_to(first_inv, (BLK, 128))
    finish(begin(sems, 0, (norm_own, norm), (hat_own, hat)))


def load_feed(w_mine, w_other, weights, sems, order):
    core = places()[2]
    loads = {}
    for k in order:
        rows = pl.ds(48 * k, 48)
        loads[k] = begin(
            sems,
            2 * k,
            (w_mine.at[:, rows], weights.at[k, :, core]),
            (w_other.at[:, rows], weights.at[k, :, 1 - core]),
        )
    return loads


def feed_kernel(mine, other, w_mine, w_other, vectors, activ, slope, keep, send, weights, sems):
    loads = load_feed(w_mine, w_other, weights, sems, (2, 0, 3, 1))
    rows = jnp.concatenate([mine[...], other[...]], axis=0)
    b_up = jnp.where(lax.rem(places()[1], 2) == 0, vectors[8:10], vectors[10:12])
    total = None
    for e in range(2):
        finish(loads[2 + e])
        up = nn(rows, weights[2 + e].reshape(D, D)) + b_up[e : e + 1, :]
        erf = lax.erf(up * root_half)
        low = (0.5 * up * (1.0 + erf)).astype(bf16)
        activ[:, D * e : D * e + D] = low
        slope[:, D * e : D * e + D] = (
            0.5 * (1.0 + erf) + up * jnp.exp(-0.5 * up * up) * inv_root_tau
        ).astype(bf16)
        finish(loads[e])
        part = nn(low, weights[e].reshape(D, D))
        total = part if total is None else total + part
    keep[...] = total[:BLK]
    send[...] = total[BLK:].astype(bf16)


def second_kernel(norm, keep, came, vectors, out_grad, layer_out, cot, low, sums):
    second_sum = norm[...] + (keep[...] + came[...].astype(f32)) + vectors[3:4]
    second_hat, second_inv = centred(second_sum)
    layer_out[...] = (second_hat * vectors[6:7] + vectors[7:8]).astype(bf16)
    out_cot = out_grad[...].astype(f32)
    second_cot = norm_back(out_cot * vectors[6:7], second_hat, second_inv)
    cot[...] = second_cot
    down_cot = second_cot.astype(bf16)
    low[...] = down_cot
    sums[0:1] = jnp.sum(down_cot.astype(f32), axis=0, keepdims=True)
    sums[1:2] = jnp.sum(out_cot * second_hat, axis=0, keepdims=True)
    sums[2:3] = jnp.sum(out_cot, axis=0, keepdims=True)


def feed_back_kernel(mine, other, w_mine, w_other, slope, up_cot, keep, send, sums, weights, sems):
    loads = load_feed(w_mine, w_other, weights, sems, (0, 2, 1, 3))
    rows = jnp.concatenate([mine[...], other[...]], axis=0)
    total = None
    for e in range(2):
        finish(loads[e] + loads[2 + e])
        w_down = weights[e].reshape(D, D)
        w_up = weights[2 + e].reshape(D, D)
        low = (nt(rows, w_down) * slope[:, D * e : D * e + D].astype(f32)).astype(bf16)
        up_cot[:, D * e : D * e + D] = low
        sums[e : e + 1, :] = jnp.sum(low.astype(f32), axis=0, keepdims=True)
        part = nt(low, w_up)
        total = part if total is None else total + part
    keep[...] = total[:BLK]
    send[...] = total[BLK:].astype(bf16)


def feed_grad_kernel(mine, other, low_mine, low_other, activ, up_cot, keep, send, packed, sems):
    xh, zed, core = places()
    down_cot = jnp.concatenate([mine[...], other[...]], axis=0)
    first_low = jnp.concatenate([low_mine[...], low_other[...]], axis=0)
    for e in range(2):
        down = tn(activ[:, D * e : D * e + D], down_cot).astype(bf16)
        up = tn(first_low, up_cot[:, D * e : D * e + D]).astype(bf16)
        for f in range(F):
            slot = core if f % 2 == 0 else 1 - core
            packed[slot, f // 2, 48 * e : 48 * e + 48, :] = down[48 * f : 48 * f + 48]
            packed[slot, f // 2, 96 + 48 * e : 144 + 48 * e, :] = up[48 * f : 48 * f + 48]
    finish(begin(sems, 0, (packed.at[1], send), (packed.at[0], keep)))


def first_back_kernel(
    cot, keep, came, vectors, hat, w_mine, w_other, mix0, mix1, mix2, mix3,
    input_cot, grad_keep, grad_send, back0, back1, back2, back3, sums,
    weights, mixes, hats, total_own, back, packed, sems,
):
    xh, zed, core = places()
    load_hat = begin(sems, 0, (hat, hats))
    loads = begin(sems, 1, *head_rows(w_mine, w_other, weights, 48))
    late = begin(sems, 3, *((mix, mixes.at[k]) for k, mix in enumerate((mix0, mix1, mix2, mix3))))
    first_cot = cot[...] + (keep[...] + came[...].astype(f32))
    finish(load_hat)
    first_hat = hats[:, :D]
    total = norm_back(first_cot * vectors[4:5], first_hat, hats[:, D : D + 1])
    total_own[...] = total
    attend_cot = total.astype(bf16)
    finish(loads)
    stores = begin(sems, 7, (total_own, input_cot))
    for k, out in enumerate((back0, back1, back2, back3)):
        back[k] = nt(attend_cot, weights[pl.ds(2 * (zed ^ k), 2)].reshape(WIDE, D)).astype(bf16)
        stores += begin(sems, 8 + k, (back.at[k], out))
    finish(late)
    for k in range(4):
        grads = tn(mixes[k], attend_cot).astype(bf16)
        for j in range(4):
            slot = core if j % 2 == 0 else 1 - core
            packed[slot, 2 * (zed ^ k) + j // 2] = grads[48 * j : 48 * j + 48]
    stores += begin(sems, 12, (packed.at[1], grad_send), (packed.at[0], grad_keep))
    sums[0:1] = jnp.sum(attend_cot.astype(f32), axis=0, keepdims=True)
    sums[1:2] = jnp.sum(first_cot * first_hat, axis=0, keepdims=True)
    sums[2:3] = jnp.sum(first_cot, axis=0, keepdims=True)
    finish(stores)


def pair_kernel(feed_keep, feed_came, out_keep, out_came, pair):
    pair[:, 0:192, :] = (feed_keep[...].astype(f32) + feed_came[...].astype(f32)).astype(bf16)
    pair[:, 192:240, :] = (out_keep[...].astype(f32) + out_came[...].astype(f32)).astype(bf16)


def feed_sum_kernel(parts, out0, out1, out2, out3, slots, sems):
    xh, zed, core = places()
    member = 2 * lax.div(zed, 2) + xh
    for m in range(4):
        rows = 64 if m < 3 else 48
        total = parts[0, 64 * m : 64 * m + rows, :].astype(f32)
        for chip in range(1, 8):
            total += parts[chip, 64 * m : 64 * m + rows, :].astype(f32)
        slots[member ^ m, 0:rows, :] = total.astype(bf16)
        if rows < 64:
            slots[member ^ m, rows:64, :] = jnp.zeros((64 - rows, D), bf16)
    finish(begin(sems, 0, *((slots.at[k], out) for k, out in enumerate((out0, out1, out2, out3)))))


def last_sum_kernel(heads, part0, part1, part2, part3, copies, total, sems):
    quarter = part0[...].astype(f32)
    for part in (part1, part2, part3):
        quarter += part[...].astype(f32)
    total[0:64, :] = quarter.astype(bf16)
    whole = heads[0].astype(f32)
    for chip in range(1, 8):
        whole += heads[chip].astype(f32)
    total[64:112, :] = whole.astype(bf16)
    finish(begin(sems, 0, *((total, copies.at[k]) for k in range(NBLK))))


def unpack_kernel(every, qkv, out, up, down, vectors, bias):
    ups = []
    for h in range(2):
        quarters = [every[4 * (m // 2) + 2 * h + m % 2, 0:64, :].astype(f32) for m in range(4)]
        whole = jnp.concatenate(quarters, axis=0)
        down[96 * h : 96 * h + 96, :] = whole[0:96]
        ups.append([whole[96:144], whole[144:192]])
        out[...] = whole[192:240] if h == 0 else out[...] + whole[192:240]
    up[...] = jnp.concatenate(
        [ups[h][e][:, 48 * f : 48 * f + 48] for f in range(F) for h in range(2) for e in range(2)], axis=1
    )
    heads = [every[2 * z, 64:112, :].astype(f32) + every[2 * z + 1, 64:112, :].astype(f32) for z in range(4)]
    for t in range(3):
        qkv[:, D * t : D * t + D] = jnp.concatenate(
            [heads[z][:, WIDE * t : WIDE * t + WIDE] for z in range(4)], axis=1
        )
    both = [heads[h][:, EXTRA:] + heads[2 + h][:, EXTRA:] for h in range(2)]
    small = [jnp.transpose(jnp.concatenate([one, jnp.zeros((80, 128), f32)], axis=0)) for one in both]
    vectors[...] = (small[0] + small[1])[0:8, 0:48]
    bias[...] = jnp.concatenate([small[0][8:10], small[1][8:10]], axis=0)[:, 0:48]


CHIPS = [[i for i in range(F) if i % 2 == k] for k in range(2)]


def swap(x, axis, size, bit):
    return lax.ppermute(x, axis, [(i, i ^ bit) for i in range(size)])


def a2a(x, axis, groups=None):
    return lax.all_to_all(x, axis, 0, 0, tiled=True, axis_index_groups=groups)


def body(tokens, w_qkv, w_out, w_up, w_down, vectors, b_up, lengths, block_seq, out_grad):
    after = lax.optimization_barrier

    token_other = swap(tokens, "ctx", NBLK, 1)
    token_other, vectors = after((token_other, vectors))
    pair = jnp.stack([tokens, token_other])
    pairs = [swap(pair, "ctx", NBLK, 2 * k) for k in (1, 2, 3)]
    heads_out, feed_out = call(
        pack_kernel,
        "pack",
        (shape((8, 96, D), bf16), shape((8, 192, D), bf16)),
        [VM, VM] + [HB] * 4,
        [
            pltpu.VMEM((96, D), bf16),
            pltpu.VMEM((192, D), bf16),
            pltpu.VMEM((48, 3 * D), bf16),
            pltpu.VMEM((48, FF), bf16),
            dma(20),
        ],
        mib=56,
        flops=10**6,
        nbytes=5 * 10**6,
        out_specs=(HB, HB),
    )(vectors, b_up.reshape(1, 192), w_qkv, w_out, w_up, w_down)
    w1_mine = a2a(heads_out, "fsdp", CHIPS)
    w1_mine, feed_out, *pairs = after((w1_mine, feed_out, *pairs))
    w2_mine = a2a(feed_out, "fsdp", CHIPS)
    w1_other = swap(w1_mine, "fsdp", F, 1)

    blocks = [tokens, token_other, *pairs]
    rows, *kept, mix0, mix1, mix2, mix3 = attend(lengths, block_seq, blocks, w1_mine, w1_other)
    mixes = [mix0] + [swap(mix, "ctx", NBLK, 2 * (k + 1)) for k, mix in enumerate((mix1, mix2, mix3))]
    first_low, first_norm, first_hat = call(
        first_kernel,
        "first",
        (shape((BLK, D), bf16), shape((BLK, D)), shape((BLK, D + 128))),
        [HB] * 6 + [VM, VM],
        [
            pltpu.VMEM((8, 2, 48, D), bf16),
            pltpu.VMEM((4, BLK, WIDE), bf16),
            pltpu.VMEM((BLK, D), f32),
            pltpu.VMEM((BLK, D + 128), f32),
            dma(6),
        ],
        flops=2 * BLK * D * D,
        nbytes=4 * 10**6,
        out_specs=(VM, HB, HB),
    )(*mixes, w1_mine, w1_other, rows, tokens)
    low_other = swap(first_low, "ctx", NBLK, 2)
    w2_mine, first_norm = after((w2_mine, first_norm))
    w2_other = swap(w2_mine, "fsdp", F, 1)
    loaded = [pltpu.VMEM((4, 8, 2, 48, D), bf16), dma(8)]
    activ, slope, keep, send = call(
        feed_kernel,
        "feed",
        (shape((2 * BLK, HALF), bf16), shape((2 * BLK, HALF), bf16), shape((BLK, D)), shape((BLK, D), bf16)),
        [VM, VM, HB, HB, VM],
        loaded,
        flops=8 * BLK * D * HALF,
        nbytes=8 * 10**6,
    )(first_low, low_other, w2_mine, w2_other, rows)
    came = swap(send, "ctx", NBLK, 2)
    layer_out, second_cot, down_cot, second_sums = call(
        second_kernel,
        "second",
        (shape((BLK, D), bf16), shape((BLK, D)), shape((BLK, D), bf16), shape((3, D))),
        [VM] * 5,
        flops=10**7,
        nbytes=2 * 10**6,
    )(first_norm, keep, came, rows, out_grad)
    down_other = swap(down_cot, "ctx", NBLK, 2)
    up_cot, keep, send, up_sums = call(
        feed_back_kernel,
        "feed_back",
        (shape((2 * BLK, HALF), bf16), shape((BLK, D)), shape((BLK, D), bf16), shape((2, D))),
        [VM, VM, HB, HB, VM],
        loaded,
        flops=8 * BLK * D * HALF,
        nbytes=8 * 10**6,
    )(down_cot, down_other, w2_mine, w2_other, slope)
    came = swap(send, "ctx", NBLK, 2)
    feed_part = shape((8, 192, D), bf16)
    feed_keep, feed_send = call(
        feed_grad_kernel,
        "feed_grad",
        (feed_part, feed_part),
        [VM] * 6,
        [pltpu.VMEM((2, 8, 192, D), bf16), dma(2)],
        mib=20,
        flops=8 * BLK * D * HALF,
        nbytes=8 * 10**6,
        out_specs=(HB, HB),
    )(down_cot, down_other, first_low, low_other, activ, up_cot)
    feed_send, came = after((feed_send, came))
    feed_came = swap(feed_send, "fsdp", F, 1)
    out_part = shape((8, 48, D), bf16)
    back_part = shape((BLK, WIDE), bf16)
    input_cot, out_keep, out_send, back0, back1, back2, back3, first_sums = call(
        first_back_kernel,
        "first_back",
        (shape((BLK, D)), out_part, out_part, back_part, back_part, back_part, back_part, shape((3, D))),
        [VM] * 4 + [HB] * 7,
        [
            pltpu.VMEM((8, 2, 48, D), bf16),
            pltpu.VMEM((4, BLK, WIDE), bf16),
            pltpu.VMEM((BLK, D + 128), f32),
            pltpu.VMEM((BLK, D), f32),
            pltpu.VMEM((4, BLK, WIDE), bf16),
            pltpu.VMEM((2, 8, 48, D), bf16),
            dma(14),
        ],
        flops=4 * BLK * D * D,
        nbytes=4 * 10**6,
        out_specs=(HB,) * 7 + (VM,),
    )(second_cot, keep, came, rows, first_hat, w1_mine, w1_other, *mixes)
    feed_came, back1 = after((feed_came, back1))
    cots = [back0] + [swap(back, "ctx", NBLK, 2 * (k + 1)) for k, back in enumerate((back1, back2, back3))]
    out_came = swap(out_send, "fsdp", F, 1)

    def add(one, two):
        return (one.astype(f32) + two.astype(f32)).astype(bf16)

    feed_pair = call(pair_kernel, "pair", shape((8, 240, D), bf16), [VM] * 4, mib=56, flops=10**6, nbytes=9 * 10**6)(
        feed_keep, feed_came, out_keep, out_came
    )
    feed_parts = a2a(feed_pair, "fsdp", CHIPS)
    *head_cots, part0, part1, part2, part3 = attend_back(block_seq, w1_mine, w1_other, cots, kept)
    partials = (part0, part1, part2, part3)
    head_keep, head_send = head_grad(blocks, head_cots, (first_sums, second_sums, up_sums))
    head_came = swap(head_send, "fsdp", F, 1)
    token_parts = [swap(partials[k], "ctx", NBLK, 2 * k) for k in (1, 2, 3)]
    head_pair, *token_parts = after((add(head_keep, head_came), *token_parts))
    head_parts = a2a(head_pair, "fsdp", CHIPS)

    part0, part1, part2, part3 = call(
        feed_sum_kernel,
        "feed_sum",
        (shape((64, D), bf16),) * 4,
        [VM],
        [pltpu.VMEM((4, 64, D), bf16), dma(4)],
        mib=56,
        flops=10**6,
        nbytes=3 * 10**6,
        out_specs=(HB,) * 4,
    )(feed_parts)
    parts = [part0] + [swap(part, "ctx", NBLK, bit) for part, bit in ((part1, 1), (part2, 4), (part3, 5))]
    copies = call(
        last_sum_kernel,
        "last_sum",
        shape((NBLK, 112, D), bf16),
        [VM] * 5,
        [pltpu.VMEM((112, D), bf16), dma(NBLK)],
        mib=56,
        flops=10**6,
        nbytes=4 * 10**6,
        out_specs=HB,
    )(head_parts, *parts)
    by_z = partials[0].astype(f32)
    for part in token_parts:
        by_z += part.astype(f32)
    by_z = by_z.astype(bf16)
    tokens_grad = input_cot + by_z[0].astype(f32) + swap(by_z[1], "ctx", NBLK, 1).astype(f32)
    every = a2a(copies, "ctx")
    qkv_grad, out_grad_w, up_grad, down_grad, vectors_grad, bias_grad = call(
        unpack_kernel,
        "unpack",
        (shape((48, 3 * D)), shape((48, D)), shape((48, FF)), shape((192, D)), shape((8, 48)), shape((4, 48))),
        [VM],
        flops=10**6,
        nbytes=4 * 10**6,
    )(every)
    return (layer_out, tokens_grad, qkv_grad, out_grad_w, up_grad, down_grad, vectors_grad, bias_grad.reshape(192))


def solution(mesh):
    by_token = P(("fsdp", "ctx"), None)
    by_row = P("fsdp", None)
    in_specs = (
        by_token, by_row, by_row, by_row, by_row, P(None, "fsdp"), P("fsdp"), by_row, by_row, by_token,
    )
    out_specs = (by_token, by_token, by_row, by_row, by_row, by_row, P(None, "fsdp"), P("fsdp"))
    return jax.shard_map(body, mesh=mesh, in_specs=in_specs, out_specs=out_specs, check_vma=False)
```

```python
import jax
import jax.numpy as jnp
from jax import lax
from jax.experimental import pallas as pl
from jax.experimental.pallas import tpu as pltpu
from jax.sharding import PartitionSpec as P

D = 768
HD = 64
BLK = 128
NBLK = 8
SEQS = 3
SLOTS = 4
LOCAL = 3
WIDE = LOCAL * HD
FF = 3072
HALF = FF // 2
F = 16

epsilon = 1e-12
masked_fill = -1e30
root_half = 0.7071067811865476
inv_root_tau = 0.3989422804014327

bf16 = jnp.bfloat16
f32 = jnp.float32

VM = pl.BlockSpec(memory_space=pltpu.VMEM)
SM = pl.BlockSpec(memory_space=pltpu.SMEM)
HB = pl.BlockSpec(memory_space=pltpu.HBM)
EXTRA = 640


def params(mib):
    return pltpu.CompilerParams(vmem_limit_bytes=mib * 1024 * 1024)


def nn(a, b):
    return lax.dot_general(a, b, (((1,), (0,)), ((), ())), preferred_element_type=f32)


def nt(a, b):
    return lax.dot_general(a, b, (((1,), (1,)), ((), ())), preferred_element_type=f32)


def tn(a, b):
    return lax.dot_general(a, b, (((0,), (0,)), ((), ())), preferred_element_type=f32)


def call(kernel, name, out_shape, in_specs, scratch=(), flops=0, nbytes=0, out_specs=None, mib=16):
    return pl.pallas_call(
        kernel,
        out_shape=out_shape,
        in_specs=in_specs,
        out_specs=jax.tree.map(lambda _: VM, out_shape) if out_specs is None else out_specs,
        scratch_shapes=list(scratch),
        compiler_params=params(mib),
        cost_estimate=pl.CostEstimate(flops=flops, bytes_accessed=nbytes, transcendentals=0),
        name=name,
    )


def shape(dims, dtype=f32):
    return jax.ShapeDtypeStruct(dims, dtype)


def places():
    place = lax.axis_index("ctx")
    return lax.rem(place, 2), lax.div(place, 2), lax.rem(lax.axis_index("fsdp"), 2)


def begin(sems, first, *pairs):
    copies = [pltpu.make_async_copy(a, b, sems.at[first + k]) for k, (a, b) in enumerate(pairs)]
    for copy in copies:
        copy.start()
    return copies


def finish(copies):
    for copy in copies:
        copy.wait()


def dma(n):
    return pltpu.SemaphoreType.DMA((n,))


def head_rows(w_mine, w_other, weights, row):
    core = places()[2]
    return (
        (w_mine.at[:, pl.ds(row, 48)], weights.at[:, core]),
        (w_other.at[:, pl.ds(row, 48)], weights.at[:, 1 - core]),
    )


def token_rows(tokens, other, pairs, x):
    xh, zed, _ = places()
    moves = [(tokens, x.at[2 * zed + xh]), (other, x.at[2 * zed + 1 - xh])]
    for k, pair in enumerate(pairs):
        z = zed ^ (k + 1)
        moves += [(pair.at[0], x.at[2 * z + xh]), (pair.at[1], x.at[2 * z + 1 - xh])]
    return moves


def slot_table(block_seq, table):
    xh, _, _ = places()
    for i in range(4):
        own = block_seq[0, 2 * i + xh]
        for k in range(SLOTS):
            table[SLOTS * i + k] = 0
        count = jnp.int32(0)
        for b in range(NBLK):
            same = block_seq[0, b] == own

            @pl.when(same)
            def _(i=i, b=b, count=count):
                table[SLOTS * i + jnp.minimum(count, SLOTS - 1)] = b

            count = count + same.astype(jnp.int32)


def attend_kernel(lengths, block_seq, tokens, other, pair1, pair2, pair3, w_mine, w_other, rows, *refs):
    kept_out, sends, refs = refs[:4], refs[4:8], refs[8:]
    x, own, weights, chances, query, keys, values, mixture, table, sems = refs
    loads = begin(sems, 0, *token_rows(tokens, other, (pair1, pair2, pair3), x))
    loads += begin(sems, 13, (tokens, own.at[places()[1]]))
    loads += begin(
        sems, 14, *((pair.at[0], own.at[places()[1] ^ (k + 1)]) for k, pair in enumerate((pair1, pair2, pair3)))
    )
    loads += begin(sems, 8, *head_rows(w_mine, w_other, weights, 0))
    slot_table(block_seq, table)
    xh, zed, core = places()
    finish(loads)
    w = weights[...].reshape(D, D)
    rows[...] = jnp.transpose(w[:, EXTRA:].astype(f32))[:16]
    bias = jnp.zeros((2, WIDE), f32)
    for z in range(4):
        bias = jnp.where(zed == z, rows[0:2, WIDE * z : WIDE * z + WIDE], bias)
    xs = x[...].reshape(NBLK * BLK, D)
    key_all = nn(xs, w[:, WIDE : 2 * WIDE]).astype(bf16)
    value_all = (nn(xs, w[:, 2 * WIDE : 3 * WIDE]) + bias[1:2, :]).astype(bf16)
    for h in range(LOCAL):
        keys[h] = key_all[:, HD * h : HD * h + HD]
        values[h] = value_all[:, HD * h : HD * h + HD]
    q_all = (nn(own[...].reshape(4 * BLK, D), w[:, :WIDE]) + bias[0:1, :]).astype(bf16) * bf16(HD**-0.5)
    for h in range(LOCAL):
        query[h] = q_all[:, HD * h : HD * h + HD]
    stores = begin(sems, 10, *zip((query, keys, values), kept_out[1:]))
    lane = lax.broadcasted_iota(jnp.int32, (1, BLK), 1)
    for i in range(4):
        length = lengths[0, block_seq[0, 2 * i + xh]]
        blank = jnp.concatenate(
            [jnp.where(lane < length - BLK * k, 0.0, masked_fill) for k in range(SLOTS)], axis=1
        )
        picks = [pl.ds(pl.multiple_of(table[SLOTS * i + k] * BLK, BLK), BLK) for k in range(SLOTS)]
        outs = []
        for h in range(LOCAL):
            key_h = jnp.concatenate([keys[h, p, :] for p in picks], axis=0)
            value_h = jnp.concatenate([values[h, p, :] for p in picks], axis=0)
            scores = nt(query[h, BLK * i : BLK * i + BLK, :], key_h) + blank
            peak = jnp.max(scores, axis=-1, keepdims=True)
            raised = jnp.exp(scores - peak)
            share = (raised * (1.0 / jnp.sum(raised, axis=-1, keepdims=True))).astype(bf16)
            chances[i, h] = share
            outs.append(nn(share, value_h))
        mixture[zed ^ i] = jnp.concatenate(outs, axis=1).astype(bf16)
        stores += begin(sems, 4 + i, (chances.at[i], kept_out[0].at[i]))
    stores += begin(sems, 0, *((mixture.at[k], out) for k, out in enumerate(sends)))
    finish(stores)


KEPT = (
    shape((4, LOCAL, BLK, SLOTS * BLK), bf16),
    shape((LOCAL, 4 * BLK, HD), bf16),
    shape((LOCAL, NBLK * BLK, HD), bf16),
    shape((LOCAL, NBLK * BLK, HD), bf16),
)
KEPT_VMEM = [pltpu.VMEM(one.shape, one.dtype) for one in KEPT]


def attend(lengths, block_seq, blocks, w_mine, w_other):
    return call(
        attend_kernel,
        "attend",
        (shape((16, D)),) + KEPT + (shape((BLK, WIDE), bf16),) * 4,
        [SM, SM] + [HB] * 7,
        [pltpu.VMEM((NBLK, BLK, D), bf16), pltpu.VMEM((4, BLK, D), bf16), pltpu.VMEM((8, 2, 48, D), bf16)]
        + KEPT_VMEM
        + [pltpu.VMEM((4, BLK, WIDE), bf16), pltpu.SMEM((4 * SLOTS,), jnp.int32), dma(17)],
        mib=56,
        flops=2 * 10**9,
        nbytes=6 * 10**6,
        out_specs=(VM,) + (HB,) * 8,
    )(lengths, block_seq, *blocks, w_mine, w_other)


def attend_back_kernel(block_seq, w_mine, w_other, *refs):
    cots, kept, refs = refs[:4], refs[4:8], refs[8:]
    query_out, key_out, value_out, part0, part1, part2, part3, weights, chances, query, keys, values = refs[:12]
    table, key_acc, value_acc, cot, partial, sems = refs[12:]
    xh, zed, core = places()
    loads = begin(sems, 0, *((one, cot.at[zed ^ k]) for k, one in enumerate(cots)))
    loads += begin(sems, 4, *zip(kept, (chances, query, keys, values)))
    late = begin(sems, 8, *head_rows(w_mine, w_other, weights, 0))
    slot_table(block_seq, table)
    key_acc[...] = jnp.zeros_like(key_acc)
    value_acc[...] = jnp.zeros_like(value_acc)
    finish(loads)
    query_cots = []
    for i in range(4):
        picks = [pl.ds(pl.multiple_of(table[SLOTS * i + k] * BLK, BLK), BLK) for k in range(SLOTS)]
        parts = []
        cot_i = cot[i]
        for h in range(LOCAL):
            key_h = jnp.concatenate([keys[h, p, :] for p in picks], axis=0)
            value_h = jnp.concatenate([values[h, p, :] for p in picks], axis=0)
            cot_h = cot_i[:, HD * h : HD * h + HD]
            share_low = chances[i, h]
            share = share_low.astype(f32)
            chance_cot = nt(cot_h, value_h)
            inner = jnp.sum(share * chance_cot, axis=-1, keepdims=True)
            score_cot = (share * (chance_cot - inner)).astype(bf16)
            parts.append(nn(score_cot, key_h))
            key_part = tn(score_cot, query[h, BLK * i : BLK * i + BLK, :])
            value_part = tn(share_low, cot_h)
            for k, p in enumerate(picks):
                key_acc[h, p, :] += key_part[BLK * k : BLK * k + BLK]
                value_acc[h, p, :] += value_part[BLK * k : BLK * k + BLK]
        query_cots.append((jnp.concatenate(parts, axis=1) * HD**-0.5).astype(bf16))
    query_cot = jnp.concatenate(query_cots, axis=0)
    key_cot = jnp.concatenate([key_acc[h] for h in range(LOCAL)], axis=1).astype(bf16)
    value_cot = jnp.concatenate([value_acc[h] for h in range(LOCAL)], axis=1).astype(bf16)
    query_out[...] = query_cot
    key_out[...] = key_cot
    value_out[...] = value_cot
    finish(late)
    w = weights[...].reshape(D, D)
    key_value = nt(key_cot, w[:, WIDE : 2 * WIDE]) + nt(value_cot, w[:, 2 * WIDE : 3 * WIDE])
    query_part = nt(query_cot, w[:, :WIDE])
    for i in range(4):
        row = BLK * 2 * i
        mine_q = query_part[BLK * i : BLK * i + BLK]
        partial[zed ^ i, 0] = (
            jnp.where(xh == 0, key_value[row : row + BLK], key_value[row + BLK : row + 2 * BLK]) + mine_q
        ).astype(bf16)
        partial[zed ^ i, 1] = jnp.where(
            xh == 0, key_value[row + BLK : row + 2 * BLK], key_value[row : row + BLK]
        ).astype(bf16)
    stores = begin(sems, 0, *((partial.at[k], out) for k, out in enumerate((part0, part1, part2, part3))))
    finish(stores)


def attend_back(block_seq, w_mine, w_other, cots, kept):
    return call(
        attend_back_kernel,
        "attend_back",
        (shape((4 * BLK, WIDE), bf16), shape((NBLK * BLK, WIDE), bf16), shape((NBLK * BLK, WIDE), bf16))
        + (shape((2, BLK, D), bf16),) * 4,
        [SM] + [HB] * 10,
        [pltpu.VMEM((8, 2, 48, D), bf16)]
        + KEPT_VMEM
        + [
            pltpu.SMEM((4 * SLOTS,), jnp.int32),
            pltpu.VMEM((LOCAL, NBLK * BLK, HD), f32),
            pltpu.VMEM((LOCAL, NBLK * BLK, HD), f32),
            pltpu.VMEM((4, BLK, WIDE), bf16),
            pltpu.VMEM((4, 2, BLK, D), bf16),
            dma(10),
        ],
        mib=56,
        flops=4 * 10**9,
        nbytes=8 * 10**6,
        out_specs=(VM,) * 3 + (HB,) * 4,
    )(block_seq, w_mine, w_other, *cots, *kept)


def head_grad_kernel(
    tokens, other, pair1, pair2, pair3, query, keys, values, first_sums, second_sums, up_sums,
    mine, send, x, packed, sems,
):
    loads = begin(sems, 0, *token_rows(tokens, other, (pair1, pair2, pair3), x))
    xh, zed, core = places()
    query_cot, key_cot, value_cot = query[...], keys[...], values[...]
    finish(loads)
    xs = x[...].reshape(NBLK * BLK, D)
    xq = jnp.concatenate([x[2 * i + xh] for i in range(4)], axis=0)
    grads = jnp.concatenate(
        [tn(xq, query_cot), tn(xs, key_cot), tn(xs, value_cot), jnp.zeros((D, EXTRA - 3 * WIDE), f32)], axis=1
    ).astype(bf16)
    lane = lax.broadcasted_iota(jnp.int32, (2, D), 1)
    edge = zed * WIDE
    inside = (lane >= edge) & (lane < edge + WIDE)
    own = jnp.concatenate(
        [
            jnp.sum(query_cot.astype(f32), axis=0, keepdims=True),
            jnp.sum(value_cot.astype(f32), axis=0, keepdims=True),
        ],
        axis=0,
    )
    own = jnp.where(inside, jnp.concatenate([own] * 4, axis=1), 0.0)
    vec = jnp.concatenate(
        [first_sums[0:1], second_sums[0:1], first_sums[1:3], second_sums[1:3], up_sums[...]], axis=0
    )
    extra = jnp.concatenate([own, vec, jnp.zeros((118, D), f32)], axis=0)
    extra = jnp.transpose(extra).astype(bf16)
    for f in range(F):
        slot = core if f % 2 == 0 else 1 - core
        packed[slot, f // 2, :, :EXTRA] = grads[48 * f : 48 * f + 48]
        packed[slot, f // 2, :, EXTRA:] = extra[48 * f : 48 * f + 48]
    stores = begin(sems, 0, (packed.at[1], send), (packed.at[0], mine))
    finish(stores)


def head_grad(blocks, cots, sums):
    half = shape((8, 48, D), bf16)
    return call(
        head_grad_kernel,
        "head_grad",
        (half, half),
        [HB] * 5 + [VM] * 6,
        [pltpu.VMEM((NBLK, BLK, D), bf16), pltpu.VMEM((2, 8, 48, D), bf16), dma(8)],
        mib=56,
        flops=2 * 10**9,
        nbytes=4 * 10**6,
        out_specs=(HB, HB),
    )(*blocks, *cots, *sums)


def centred(hidden):
    centre = hidden - jnp.mean(hidden, axis=-1, keepdims=True)
    inverse = lax.rsqrt(jnp.mean(centre * centre, axis=-1, keepdims=True) + epsilon)
    return centre * inverse, inverse


def norm_back(scaled, hat, inverse):
    return inverse * (
        scaled
        - jnp.mean(scaled, axis=-1, keepdims=True)
        - hat * jnp.mean(scaled * hat, axis=-1, keepdims=True)
    )


def pack_heads_kernel(vectors, b_up, w_qkv, w_out, copies, heads, qkv, sems):
    zed = places()[1]
    loads = begin(sems, 0, (w_qkv, qkv), (w_out, heads.at[pl.ds(48, 48)]))
    bias = b_up[...].astype(f32)
    small = jnp.concatenate([vectors[...].astype(f32)] + [bias[:, 48 * e : 48 * e + 48] for e in range(4)], axis=0)
    small = jnp.concatenate([small, jnp.zeros((12, 80), f32)], axis=1)
    small = jnp.concatenate([small, jnp.zeros((116, 128), f32)], axis=0)
    heads[0:48, EXTRA:] = jnp.transpose(small)[:48].astype(bf16)
    heads[0:48, 3 * WIDE : EXTRA] = jnp.zeros((48, EXTRA - 3 * WIDE), bf16)
    finish(loads)
    for z in range(4):

        @pl.when(zed == z)
        def _(z=z):
            heads[0:48, : 3 * WIDE] = jnp.concatenate(
                [qkv[:, D * t + WIDE * z : D * t + WIDE * z + WIDE] for t in range(3)], axis=1
            )

    finish(begin(sems, 2, *((heads, copies.at[k]) for k in range(8))))


def pack_feed_kernel(w_up, w_down, feed, feed_own, up, sems):
    half = lax.rem(places()[1], 2)
    start = pl.multiple_of(96 * half, 32)
    loads = begin(
        sems,
        0,
        (w_up, up),
        (w_down.at[pl.ds(start, 96)], feed_own.at[pl.ds(0, 96)]),
    )
    loads[0].wait()
    for h in range(2):

        @pl.when(half == h)
        def _(h=h):
            for e in range(2):
                first = 96 * h + 48 * e
                feed_own[96 + 48 * e : 144 + 48 * e, :] = jnp.concatenate(
                    [up[:, 192 * f + first : 192 * f + first + 48] for f in range(F)], axis=1
                )

    finish(loads[1:])
    finish(begin(sems, 2, *((feed_own, feed.at[k]) for k in range(8))))


def first_kernel(mix0, mix1, mix2, mix3, w_mine, w_other, vectors, tokens, low, norm, hat, *scratch):
    weights, mixes, norm_own, hat_own, sems = scratch
    xh, zed, core = places()
    loads = begin(sems, 0, *((mix, mixes.at[k]) for k, mix in enumerate((mix0, mix1, mix2, mix3))))
    loads += begin(sems, 4, *head_rows(w_mine, w_other, weights, 48))
    total = tokens[...].astype(f32) + vectors[2:3]
    finish(loads)
    for k in range(4):
        total += nn(mixes[k], weights[pl.ds(2 * (zed ^ k), 2)].reshape(WIDE, D))
    first_hat, first_inv = centred(total)
    first_norm = first_hat * vectors[4:5] + vectors[5:6]
    low[...] = first_norm.astype(bf16)
    norm_own[...] = first_norm
    hat_own[:, :D] = first_hat
    hat_own[:, D:] = jnp.broadcast_to(first_inv, (BLK, 128))
    finish(begin(sems, 0, (norm_own, norm), (hat_own, hat)))


def load_feed(w_mine, w_other, weights, sems, order):
    core = places()[2]
    loads = {}
    for k in order:
        rows = pl.ds(48 * k, 48)
        loads[k] = begin(
            sems,
            2 * k,
            (w_mine.at[:, rows], weights.at[k, :, core]),
            (w_other.at[:, rows], weights.at[k, :, 1 - core]),
        )
    return loads


def feed_kernel(mine, other, w_mine, w_other, vectors, activ, slope, keep, send, weights, sems):
    loads = load_feed(w_mine, w_other, weights, sems, (2, 0, 3, 1))
    rows = jnp.concatenate([mine[...], other[...]], axis=0)
    b_up = jnp.where(lax.rem(places()[1], 2) == 0, vectors[8:10], vectors[10:12])
    total = None
    for e in range(2):
        finish(loads[2 + e])
        up = nn(rows, weights[2 + e].reshape(D, D)) + b_up[e : e + 1, :]
        erf = lax.erf(up * root_half)
        low = (0.5 * up * (1.0 + erf)).astype(bf16)
        activ[:, D * e : D * e + D] = low
        slope[:, D * e : D * e + D] = (
            0.5 * (1.0 + erf) + up * jnp.exp(-0.5 * up * up) * inv_root_tau
        ).astype(bf16)
        finish(loads[e])
        part = nn(low, weights[e].reshape(D, D))
        total = part if total is None else total + part
    keep[...] = total[:BLK]
    send[...] = total[BLK:].astype(bf16)


def second_kernel(norm, keep, came, vectors, out_grad, layer_out, cot, low, sums):
    second_sum = norm[...] + (keep[...] + came[...].astype(f32)) + vectors[3:4]
    second_hat, second_inv = centred(second_sum)
    layer_out[...] = (second_hat * vectors[6:7] + vectors[7:8]).astype(bf16)
    out_cot = out_grad[...].astype(f32)
    second_cot = norm_back(out_cot * vectors[6:7], second_hat, second_inv)
    cot[...] = second_cot
    down_cot = second_cot.astype(bf16)
    low[...] = down_cot
    sums[0:1] = jnp.sum(down_cot.astype(f32), axis=0, keepdims=True)
    sums[1:2] = jnp.sum(out_cot * second_hat, axis=0, keepdims=True)
    sums[2:3] = jnp.sum(out_cot, axis=0, keepdims=True)


def feed_back_kernel(mine, other, w_mine, w_other, slope, up_cot, keep, send, sums, weights, sems):
    loads = load_feed(w_mine, w_other, weights, sems, (0, 2, 1, 3))
    rows = jnp.concatenate([mine[...], other[...]], axis=0)
    total = None
    for e in range(2):
        finish(loads[e] + loads[2 + e])
        w_down = weights[e].reshape(D, D)
        w_up = weights[2 + e].reshape(D, D)
        low = (nt(rows, w_down) * slope[:, D * e : D * e + D].astype(f32)).astype(bf16)
        up_cot[:, D * e : D * e + D] = low
        sums[e : e + 1, :] = jnp.sum(low.astype(f32), axis=0, keepdims=True)
        part = nt(low, w_up)
        total = part if total is None else total + part
    keep[...] = total[:BLK]
    send[...] = total[BLK:].astype(bf16)


def feed_grad_kernel(mine, other, low_mine, low_other, activ, up_cot, keep, send, packed, sems):
    xh, zed, core = places()
    down_cot = jnp.concatenate([mine[...], other[...]], axis=0)
    first_low = jnp.concatenate([low_mine[...], low_other[...]], axis=0)
    for e in range(2):
        down = tn(activ[:, D * e : D * e + D], down_cot).astype(bf16)
        up = tn(first_low, up_cot[:, D * e : D * e + D]).astype(bf16)
        for f in range(F):
            slot = core if f % 2 == 0 else 1 - core
            packed[slot, f // 2, 48 * e : 48 * e + 48, :] = down[48 * f : 48 * f + 48]
            packed[slot, f // 2, 96 + 48 * e : 144 + 48 * e, :] = up[48 * f : 48 * f + 48]
    finish(begin(sems, 0, (packed.at[1], send), (packed.at[0], keep)))


def first_back_kernel(
    cot, keep, came, vectors, hat, w_mine, w_other, mix0, mix1, mix2, mix3,
    input_cot, grad_keep, grad_send, back0, back1, back2, back3, sums,
    weights, mixes, hats, total_own, back, packed, sems,
):
    xh, zed, core = places()
    load_hat = begin(sems, 0, (hat, hats))
    loads = begin(sems, 1, *head_rows(w_mine, w_other, weights, 48))
    late = begin(sems, 3, *((mix, mixes.at[k]) for k, mix in enumerate((mix0, mix1, mix2, mix3))))
    first_cot = cot[...] + (keep[...] + came[...].astype(f32))
    finish(load_hat)
    first_hat = hats[:, :D]
    total = norm_back(first_cot * vectors[4:5], first_hat, hats[:, D : D + 1])
    total_own[...] = total
    attend_cot = total.astype(bf16)
    finish(loads)
    stores = begin(sems, 7, (total_own, input_cot))
    for k, out in enumerate((back0, back1, back2, back3)):
        back[k] = nt(attend_cot, weights[pl.ds(2 * (zed ^ k), 2)].reshape(WIDE, D)).astype(bf16)
        stores += begin(sems, 8 + k, (back.at[k], out))
    finish(late)
    for k in range(4):
        grads = tn(mixes[k], attend_cot).astype(bf16)
        for j in range(4):
            slot = core if j % 2 == 0 else 1 - core
            packed[slot, 2 * (zed ^ k) + j // 2] = grads[48 * j : 48 * j + 48]
    stores += begin(sems, 12, (packed.at[1], grad_send), (packed.at[0], grad_keep))
    sums[0:1] = jnp.sum(attend_cot.astype(f32), axis=0, keepdims=True)
    sums[1:2] = jnp.sum(first_cot * first_hat, axis=0, keepdims=True)
    sums[2:3] = jnp.sum(first_cot, axis=0, keepdims=True)
    finish(stores)


def pair_kernel(head_keep, head_came, out_keep, out_came, pair):
    pair[:, 0:48, :] = (head_keep[...].astype(f32) + head_came[...].astype(f32)).astype(bf16)
    pair[:, 48:96, :] = (out_keep[...].astype(f32) + out_came[...].astype(f32)).astype(bf16)


def feed_sum_kernel(parts, out0, out1, out2, out3, slots, sems):
    xh, zed, _ = places()
    member = 2 * lax.div(zed, 2) + xh
    for m in range(4):
        total = parts[0, 48 * m : 48 * m + 48, :].astype(f32)
        for k in range(1, 8):
            total += parts[k, 48 * m : 48 * m + 48, :].astype(f32)
        slots[member ^ m] = total.astype(bf16)
    finish(begin(sems, 0, *((slots.at[k], out) for k, out in enumerate((out0, out1, out2, out3)))))


def last_sum_kernel(heads, part0, part1, part2, part3, total):
    quarter = part0[...].astype(f32)
    for part in (part1, part2, part3):
        quarter += part[...].astype(f32)
    total[0:48, :] = quarter.astype(bf16)
    whole = heads[0].astype(f32)
    for k in range(1, 8):
        whole += heads[k].astype(f32)
    total[48:144, :] = whole.astype(bf16)


def merge_kernel(own, other, merged):
    xh = places()[0]
    merged[pl.ds(pl.multiple_of(48 * xh, 16), 48), :] = own[0:48, :]
    merged[pl.ds(pl.multiple_of(48 * (1 - xh), 16), 48), :] = other[0:48, :]
    merged[96:192, :] = (own[48:144, :].astype(f32) + other[48:144, :].astype(f32)).astype(bf16)


def unpack_kernel(one0, one1, one2, one3, qkv, out, up, down, vectors, bias, every):
    zed = places()[1]
    for k, one in enumerate((one0, one1, one2, one3)):
        every[zed ^ k] = one[...]
    ups = []
    for h in range(2):
        quarters = [every[2 * (m // 2) + h, 48 * (m % 2) : 48 * (m % 2) + 48, :].astype(f32) for m in range(4)]
        down[96 * h : 96 * h + 48, :] = quarters[0]
        down[96 * h + 48 : 96 * h + 96, :] = quarters[1]
        ups.append(quarters[2:])
    up[...] = jnp.concatenate(
        [ups[h][e][:, 48 * f : 48 * f + 48] for f in range(F) for h in range(2) for e in range(2)], axis=1
    )
    total = every[0, 144:192, :].astype(f32)
    for z in range(1, 4):
        total += every[z, 144:192, :].astype(f32)
    out[...] = total
    heads = [every[z, 96:144, :].astype(f32) for z in range(4)]
    for t in range(3):
        qkv[:, D * t : D * t + D] = jnp.concatenate(
            [heads[z][:, WIDE * t : WIDE * t + WIDE] for z in range(4)], axis=1
        )
    both = [heads[h][:, EXTRA:] + heads[2 + h][:, EXTRA:] for h in range(2)]
    small = [jnp.transpose(jnp.concatenate([one, jnp.zeros((80, 128), f32)], axis=0)) for one in both]
    vectors[...] = (small[0] + small[1])[0:8, 0:48]
    bias[...] = jnp.concatenate([small[0][8:10], small[1][8:10]], axis=0)[:, 0:48]


CHIPS = [[i for i in range(F) if i % 2 == k] for k in range(2)]


def swap(x, axis, size, bit):
    return lax.ppermute(x, axis, [(i, i ^ bit) for i in range(size)])


def a2a(x, axis, groups=None):
    return lax.all_to_all(x, axis, 0, 0, tiled=True, axis_index_groups=groups)


def body(tokens, w_qkv, w_out, w_up, w_down, vectors, b_up, lengths, block_seq, out_grad):
    after = lax.optimization_barrier

    token_other = swap(tokens, "ctx", NBLK, 1)
    heads_out = call(
        pack_heads_kernel,
        "pack_heads",
        shape((8, 96, D), bf16),
        [VM, VM, HB, HB],
        [pltpu.VMEM((96, D), bf16), pltpu.VMEM((48, 3 * D), bf16), dma(10)],
        mib=56,
        flops=10**6,
        nbytes=2 * 10**6,
        out_specs=HB,
    )(vectors, b_up.reshape(1, 192), w_qkv, w_out)
    w_up, heads_out, token_other = after((w_up, heads_out, token_other))
    pair = jnp.stack([tokens, token_other])
    pairs = [swap(pair, "ctx", NBLK, 2 * k) for k in (1, 2, 3)]
    feed_out = call(
        pack_feed_kernel,
        "pack_feed",
        shape((8, 192, D), bf16),
        [HB] * 2,
        [pltpu.VMEM((192, D), bf16), pltpu.VMEM((48, FF), bf16), dma(10)],
        mib=56,
        flops=10**6,
        nbytes=4 * 10**6,
        out_specs=HB,
    )(w_up, w_down)
    w1_mine = a2a(heads_out, "fsdp", CHIPS)
    w1_mine, feed_out, *pairs = after((w1_mine, feed_out, *pairs))
    w2_mine = a2a(feed_out, "fsdp", CHIPS)
    w1_other = swap(w1_mine, "fsdp", F, 1)

    blocks = [tokens, token_other, *pairs]
    rows, *kept, mix0, mix1, mix2, mix3 = attend(lengths, block_seq, blocks, w1_mine, w1_other)
    mixes = [mix0] + [swap(mix, "ctx", NBLK, 2 * (k + 1)) for k, mix in enumerate((mix1, mix2, mix3))]
    first_low, first_norm, first_hat = call(
        first_kernel,
        "first",
        (shape((BLK, D), bf16), shape((BLK, D)), shape((BLK, D + 128))),
        [HB] * 6 + [VM, VM],
        [
            pltpu.VMEM((8, 2, 48, D), bf16),
            pltpu.VMEM((4, BLK, WIDE), bf16),
            pltpu.VMEM((BLK, D), f32),
            pltpu.VMEM((BLK, D + 128), f32),
            dma(6),
        ],
        mib=56,
        flops=2 * BLK * D * D,
        nbytes=4 * 10**6,
        out_specs=(VM, HB, HB),
    )(*mixes, w1_mine, w1_other, rows, tokens)
    low_other = swap(first_low, "ctx", NBLK, 2)
    w2_mine, first_norm = after((w2_mine, first_norm))
    w2_other = swap(w2_mine, "fsdp", F, 1)
    loaded = [pltpu.VMEM((4, 8, 2, 48, D), bf16), dma(8)]
    activ, slope, keep, send = call(
        feed_kernel,
        "feed",
        (shape((2 * BLK, HALF), bf16), shape((2 * BLK, HALF), bf16), shape((BLK, D)), shape((BLK, D), bf16)),
        [VM, VM, HB, HB, VM],
        loaded,
        flops=8 * BLK * D * HALF,
        nbytes=8 * 10**6,
    )(first_low, low_other, w2_mine, w2_other, rows)
    came = swap(send, "ctx", NBLK, 2)
    layer_out, second_cot, down_cot, second_sums = call(
        second_kernel,
        "second",
        (shape((BLK, D), bf16), shape((BLK, D)), shape((BLK, D), bf16), shape((3, D))),
        [VM] * 5,
        flops=10**7,
        nbytes=2 * 10**6,
    )(first_norm, keep, came, rows, out_grad)
    down_other = swap(down_cot, "ctx", NBLK, 2)
    up_cot, keep, send, up_sums = call(
        feed_back_kernel,
        "feed_back",
        (shape((2 * BLK, HALF), bf16), shape((BLK, D)), shape((BLK, D), bf16), shape((2, D))),
        [VM, VM, HB, HB, VM],
        loaded,
        flops=8 * BLK * D * HALF,
        nbytes=8 * 10**6,
    )(down_cot, down_other, w2_mine, w2_other, slope)
    came = swap(send, "ctx", NBLK, 2)
    feed_part = shape((8, 192, D), bf16)
    feed_keep, feed_send = call(
        feed_grad_kernel,
        "feed_grad",
        (feed_part, feed_part),
        [VM] * 6,
        [pltpu.VMEM((2, 8, 192, D), bf16), dma(2)],
        mib=20,
        flops=8 * BLK * D * HALF,
        nbytes=8 * 10**6,
        out_specs=(HB, HB),
    )(down_cot, down_other, first_low, low_other, activ, up_cot)
    feed_send, came = after((feed_send, came))
    feed_came = swap(feed_send, "fsdp", F, 1)
    out_part = shape((8, 48, D), bf16)
    back_part = shape((BLK, WIDE), bf16)
    input_cot, out_keep, out_send, back0, back1, back2, back3, first_sums = call(
        first_back_kernel,
        "first_back",
        (shape((BLK, D)), out_part, out_part, back_part, back_part, back_part, back_part, shape((3, D))),
        [VM] * 4 + [HB] * 7,
        [
            pltpu.VMEM((8, 2, 48, D), bf16),
            pltpu.VMEM((4, BLK, WIDE), bf16),
            pltpu.VMEM((BLK, D + 128), f32),
            pltpu.VMEM((BLK, D), f32),
            pltpu.VMEM((4, BLK, WIDE), bf16),
            pltpu.VMEM((2, 8, 48, D), bf16),
            dma(14),
        ],
        flops=4 * BLK * D * D,
        nbytes=4 * 10**6,
        out_specs=(HB,) * 7 + (VM,),
    )(second_cot, keep, came, rows, first_hat, w1_mine, w1_other, *mixes)
    def add(one, two):
        return (one.astype(f32) + two.astype(f32)).astype(bf16)

    feed_pair, back1, back2, back3 = after((add(feed_keep, feed_came), back1, back2, back3))
    feed_parts = a2a(feed_pair, "fsdp", CHIPS)
    cots = [back0] + [swap(back, "ctx", NBLK, 2 * (k + 1)) for k, back in enumerate((back1, back2, back3))]
    out_came = swap(out_send, "fsdp", F, 1)

    *head_cots, part0, part1, part2, part3 = attend_back(block_seq, w1_mine, w1_other, cots, kept)
    partials = (part0, part1, part2, part3)
    head_keep, head_send = head_grad(blocks, head_cots, (first_sums, second_sums, up_sums))
    head_came = swap(head_send, "fsdp", F, 1)
    token_parts = [swap(partials[k], "ctx", NBLK, 2 * k) for k in (1, 2, 3)]
    pair = call(pair_kernel, "pair", shape((8, 96, D), bf16), [VM] * 4, flops=10**6, nbytes=4 * 10**6)(
        head_keep, head_came, out_keep, out_came
    )
    head_parts = a2a(pair, "fsdp", CHIPS)

    part0, part1, part2, part3 = call(
        feed_sum_kernel,
        "feed_sum",
        (shape((48, D), bf16),) * 4,
        [VM],
        [pltpu.VMEM((4, 48, D), bf16), dma(4)],
        mib=56,
        flops=10**6,
        nbytes=3 * 10**6,
        out_specs=(HB,) * 4,
    )(feed_parts)
    parts = [part0] + [swap(part, "ctx", NBLK, bit) for part, bit in ((part1, 1), (part2, 4), (part3, 5))]
    head_parts, token_parts, parts = after((head_parts, token_parts, parts))
    total = call(last_sum_kernel, "last_sum", shape((144, D), bf16), [VM] * 5, flops=10**6, nbytes=2 * 10**6)(
        head_parts, *parts
    )
    merged = call(merge_kernel, "merge", shape((192, D), bf16), [VM] * 2, flops=10**6, nbytes=10**6)(
        total, swap(total, "ctx", NBLK, 1)
    )
    every = [merged] + [swap(merged, "ctx", NBLK, 2 * k) for k in (1, 2, 3)]
    by_z = partials[0].astype(f32)
    for part in token_parts:
        by_z += part.astype(f32)
    by_z = by_z.astype(bf16)
    tokens_grad = input_cot + by_z[0].astype(f32) + swap(by_z[1], "ctx", NBLK, 1).astype(f32)
    qkv_grad, out_grad_w, up_grad, down_grad, vectors_grad, bias_grad = call(
        unpack_kernel,
        "unpack",
        (shape((48, 3 * D)), shape((48, D)), shape((48, FF)), shape((192, D)), shape((8, 48)), shape((4, 48))),
        [VM] * 4,
        [pltpu.VMEM((4, 192, D), bf16)],
        flops=10**6,
        nbytes=4 * 10**6,
    )(*every)
    return (layer_out, tokens_grad, qkv_grad, out_grad_w, up_grad, down_grad, vectors_grad, bias_grad.reshape(192))


def solution(mesh):
    by_token = P(("fsdp", "ctx"), None)
    by_row = P("fsdp", None)
    in_specs = (
        by_token, by_row, by_row, by_row, by_row, P(None, "fsdp"), P("fsdp"), by_row, by_row, by_token,
    )
    out_specs = (by_token, by_token, by_row, by_row, by_row, by_row, P(None, "fsdp"), P("fsdp"))
    return jax.shard_map(body, mesh=mesh, in_specs=in_specs, out_specs=out_specs, check_vma=False)
```

```python
import jax
import jax.numpy as jnp
from jax import lax
from jax.experimental import pallas as pl
from jax.experimental.pallas import tpu as pltpu
from jax.sharding import PartitionSpec as P

D = 768
HD = 64
BLK = 128
NBLK = 8
SEQS = 3
SLOTS = 4
LOCAL = 3
WIDE = LOCAL * HD
FF = 3072
HALF = FF // 2
F = 16

epsilon = 1e-12
masked_fill = -1e30
root_half = 0.7071067811865476
inv_root_tau = 0.3989422804014327

bf16 = jnp.bfloat16
f32 = jnp.float32

VM = pl.BlockSpec(memory_space=pltpu.VMEM)
SM = pl.BlockSpec(memory_space=pltpu.SMEM)
HB = pl.BlockSpec(memory_space=pltpu.HBM)
EXTRA = 640


def params(mib):
    return pltpu.CompilerParams(vmem_limit_bytes=mib * 1024 * 1024)


def nn(a, b):
    return lax.dot_general(a, b, (((1,), (0,)), ((), ())), preferred_element_type=f32)


def nt(a, b):
    return lax.dot_general(a, b, (((1,), (1,)), ((), ())), preferred_element_type=f32)


def tn(a, b):
    return lax.dot_general(a, b, (((0,), (0,)), ((), ())), preferred_element_type=f32)


def call(kernel, name, out_shape, in_specs, scratch=(), flops=0, nbytes=0, out_specs=None, mib=16):
    return pl.pallas_call(
        kernel,
        out_shape=out_shape,
        in_specs=in_specs,
        out_specs=jax.tree.map(lambda _: VM, out_shape) if out_specs is None else out_specs,
        scratch_shapes=list(scratch),
        compiler_params=params(mib),
        cost_estimate=pl.CostEstimate(flops=flops, bytes_accessed=nbytes, transcendentals=0),
        name=name,
    )


def shape(dims, dtype=f32):
    return jax.ShapeDtypeStruct(dims, dtype)


def places():
    place = lax.axis_index("ctx")
    return lax.rem(place, 2), lax.div(place, 2), lax.rem(lax.axis_index("fsdp"), 2)


def begin(sems, first, *pairs):
    copies = [pltpu.make_async_copy(a, b, sems.at[first + k]) for k, (a, b) in enumerate(pairs)]
    for copy in copies:
        copy.start()
    return copies


def finish(copies):
    for copy in copies:
        copy.wait()


def dma(n):
    return pltpu.SemaphoreType.DMA((n,))


def head_rows(w_mine, w_other, weights, row):
    core = places()[2]
    return (
        (w_mine.at[:, pl.ds(row, 48)], weights.at[:, core]),
        (w_other.at[:, pl.ds(row, 48)], weights.at[:, 1 - core]),
    )


def token_rows(tokens, other, pairs, x):
    xh, zed, _ = places()
    moves = [(tokens, x.at[2 * zed + xh]), (other, x.at[2 * zed + 1 - xh])]
    for k, pair in enumerate(pairs):
        z = zed ^ (k + 1)
        moves += [(pair.at[0], x.at[2 * z + xh]), (pair.at[1], x.at[2 * z + 1 - xh])]
    return moves


def slot_table(block_seq, table):
    xh, _, _ = places()
    for i in range(4):
        own = block_seq[0, 2 * i + xh]
        for k in range(SLOTS):
            table[SLOTS * i + k] = 0
        count = jnp.int32(0)
        for b in range(NBLK):
            same = block_seq[0, b] == own

            @pl.when(same)
            def _(i=i, b=b, count=count):
                table[SLOTS * i + jnp.minimum(count, SLOTS - 1)] = b

            count = count + same.astype(jnp.int32)


def attend_kernel(lengths, block_seq, tokens, other, pair1, pair2, pair3, w_mine, w_other, rows, *refs):
    kept_out, sends, refs = refs[:4], refs[4:8], refs[8:]
    x, own, weights, chances, query, keys, values, mixture, table, sems = refs
    loads = begin(sems, 0, *token_rows(tokens, other, (pair1, pair2, pair3), x))
    loads += begin(sems, 13, (tokens, own.at[places()[1]]))
    loads += begin(
        sems, 14, *((pair.at[0], own.at[places()[1] ^ (k + 1)]) for k, pair in enumerate((pair1, pair2, pair3)))
    )
    loads += begin(sems, 8, *head_rows(w_mine, w_other, weights, 0))
    slot_table(block_seq, table)
    xh, zed, core = places()
    finish(loads)
    w = weights[...].reshape(D, D)
    rows[...] = jnp.transpose(w[:, EXTRA:].astype(f32))[:16]
    bias = jnp.zeros((2, WIDE), f32)
    for z in range(4):
        bias = jnp.where(zed == z, rows[0:2, WIDE * z : WIDE * z + WIDE], bias)
    xs = x[...].reshape(NBLK * BLK, D)
    key_all = nn(xs, w[:, WIDE : 2 * WIDE]).astype(bf16)
    value_all = (nn(xs, w[:, 2 * WIDE : 3 * WIDE]) + bias[1:2, :]).astype(bf16)
    for h in range(LOCAL):
        keys[h] = key_all[:, HD * h : HD * h + HD]
        values[h] = value_all[:, HD * h : HD * h + HD]
    q_all = (nn(own[...].reshape(4 * BLK, D), w[:, :WIDE]) + bias[0:1, :]).astype(bf16) * bf16(HD**-0.5)
    for h in range(LOCAL):
        query[h] = q_all[:, HD * h : HD * h + HD]
    stores = begin(sems, 10, *zip((query, keys, values), kept_out[1:]))
    lane = lax.broadcasted_iota(jnp.int32, (1, BLK), 1)
    for i in range(4):
        length = lengths[0, block_seq[0, 2 * i + xh]]
        blank = jnp.concatenate(
            [jnp.where(lane < length - BLK * k, 0.0, masked_fill) for k in range(SLOTS)], axis=1
        )
        picks = [pl.ds(pl.multiple_of(table[SLOTS * i + k] * BLK, BLK), BLK) for k in range(SLOTS)]
        outs = []
        for h in range(LOCAL):
            key_h = jnp.concatenate([keys[h, p, :] for p in picks], axis=0)
            value_h = jnp.concatenate([values[h, p, :] for p in picks], axis=0)
            scores = nt(query[h, BLK * i : BLK * i + BLK, :], key_h) + blank
            peak = jnp.max(scores, axis=-1, keepdims=True)
            raised = jnp.exp(scores - peak)
            share = (raised * (1.0 / jnp.sum(raised, axis=-1, keepdims=True))).astype(bf16)
            chances[i, h] = share
            outs.append(nn(share, value_h))
        mixture[zed ^ i] = jnp.concatenate(outs, axis=1).astype(bf16)
        stores += begin(sems, 4 + i, (chances.at[i], kept_out[0].at[i]))
    stores += begin(sems, 0, *((mixture.at[k], out) for k, out in enumerate(sends)))
    finish(stores)


KEPT = (
    shape((4, LOCAL, BLK, SLOTS * BLK), bf16),
    shape((LOCAL, 4 * BLK, HD), bf16),
    shape((LOCAL, NBLK * BLK, HD), bf16),
    shape((LOCAL, NBLK * BLK, HD), bf16),
)
KEPT_VMEM = [pltpu.VMEM(one.shape, one.dtype) for one in KEPT]


def attend(lengths, block_seq, blocks, w_mine, w_other):
    return call(
        attend_kernel,
        "attend",
        (shape((16, D)),) + KEPT + (shape((BLK, WIDE), bf16),) * 4,
        [SM, SM] + [HB] * 7,
        [pltpu.VMEM((NBLK, BLK, D), bf16), pltpu.VMEM((4, BLK, D), bf16), pltpu.VMEM((8, 2, 48, D), bf16)]
        + KEPT_VMEM
        + [pltpu.VMEM((4, BLK, WIDE), bf16), pltpu.SMEM((4 * SLOTS,), jnp.int32), dma(17)],
        mib=56,
        flops=2 * 10**9,
        nbytes=6 * 10**6,
        out_specs=(VM,) + (HB,) * 8,
    )(lengths, block_seq, *blocks, w_mine, w_other)


def attend_back_kernel(block_seq, w_mine, w_other, *refs):
    cots, kept, refs = refs[:4], refs[4:8], refs[8:]
    query_out, key_out, value_out, part0, part1, part2, part3, weights, chances, query, keys, values = refs[:12]
    table, key_acc, value_acc, cot, partial, sems = refs[12:]
    xh, zed, core = places()
    loads = begin(sems, 0, *((one, cot.at[zed ^ k]) for k, one in enumerate(cots)))
    loads += begin(sems, 4, *zip(kept, (chances, query, keys, values)))
    late = begin(sems, 8, *head_rows(w_mine, w_other, weights, 0))
    slot_table(block_seq, table)
    key_acc[...] = jnp.zeros_like(key_acc)
    value_acc[...] = jnp.zeros_like(value_acc)
    finish(loads)
    query_cots = []
    for i in range(4):
        picks = [pl.ds(pl.multiple_of(table[SLOTS * i + k] * BLK, BLK), BLK) for k in range(SLOTS)]
        parts = []
        cot_i = cot[i]
        for h in range(LOCAL):
            key_h = jnp.concatenate([keys[h, p, :] for p in picks], axis=0)
            value_h = jnp.concatenate([values[h, p, :] for p in picks], axis=0)
            cot_h = cot_i[:, HD * h : HD * h + HD]
            share_low = chances[i, h]
            share = share_low.astype(f32)
            chance_cot = nt(cot_h, value_h)
            inner = jnp.sum(share * chance_cot, axis=-1, keepdims=True)
            score_cot = (share * (chance_cot - inner)).astype(bf16)
            parts.append(nn(score_cot, key_h))
            key_part = tn(score_cot, query[h, BLK * i : BLK * i + BLK, :])
            value_part = tn(share_low, cot_h)
            for k, p in enumerate(picks):
                key_acc[h, p, :] += key_part[BLK * k : BLK * k + BLK]
                value_acc[h, p, :] += value_part[BLK * k : BLK * k + BLK]
        query_cots.append((jnp.concatenate(parts, axis=1) * HD**-0.5).astype(bf16))
    query_cot = jnp.concatenate(query_cots, axis=0)
    key_cot = jnp.concatenate([key_acc[h] for h in range(LOCAL)], axis=1).astype(bf16)
    value_cot = jnp.concatenate([value_acc[h] for h in range(LOCAL)], axis=1).astype(bf16)
    query_out[...] = query_cot
    key_out[...] = key_cot
    value_out[...] = value_cot
    finish(late)
    w = weights[...].reshape(D, D)
    key_value = nt(key_cot, w[:, WIDE : 2 * WIDE]) + nt(value_cot, w[:, 2 * WIDE : 3 * WIDE])
    query_part = nt(query_cot, w[:, :WIDE])
    for i in range(4):
        row = BLK * 2 * i
        mine_q = query_part[BLK * i : BLK * i + BLK]
        partial[zed ^ i, 0] = (
            jnp.where(xh == 0, key_value[row : row + BLK], key_value[row + BLK : row + 2 * BLK]) + mine_q
        ).astype(bf16)
        partial[zed ^ i, 1] = jnp.where(
            xh == 0, key_value[row + BLK : row + 2 * BLK], key_value[row : row + BLK]
        ).astype(bf16)
    stores = begin(sems, 0, *((partial.at[k], out) for k, out in enumerate((part0, part1, part2, part3))))
    finish(stores)


def attend_back(block_seq, w_mine, w_other, cots, kept):
    return call(
        attend_back_kernel,
        "attend_back",
        (shape((4 * BLK, WIDE), bf16), shape((NBLK * BLK, WIDE), bf16), shape((NBLK * BLK, WIDE), bf16))
        + (shape((2, BLK, D), bf16),) * 4,
        [SM] + [HB] * 10,
        [pltpu.VMEM((8, 2, 48, D), bf16)]
        + KEPT_VMEM
        + [
            pltpu.SMEM((4 * SLOTS,), jnp.int32),
            pltpu.VMEM((LOCAL, NBLK * BLK, HD), f32),
            pltpu.VMEM((LOCAL, NBLK * BLK, HD), f32),
            pltpu.VMEM((4, BLK, WIDE), bf16),
            pltpu.VMEM((4, 2, BLK, D), bf16),
            dma(10),
        ],
        mib=56,
        flops=4 * 10**9,
        nbytes=8 * 10**6,
        out_specs=(VM,) * 3 + (HB,) * 4,
    )(block_seq, w_mine, w_other, *cots, *kept)


def head_grad_kernel(
    tokens, other, pair1, pair2, pair3, query, keys, values, first_sums, second_sums, up_sums,
    mine, send, x, packed, sems,
):
    loads = begin(sems, 0, *token_rows(tokens, other, (pair1, pair2, pair3), x))
    xh, zed, core = places()
    query_cot, key_cot, value_cot = query[...], keys[...], values[...]
    finish(loads)
    xs = x[...].reshape(NBLK * BLK, D)
    xq = jnp.concatenate([x[2 * i + xh] for i in range(4)], axis=0)
    grads = jnp.concatenate(
        [tn(xq, query_cot), tn(xs, key_cot), tn(xs, value_cot), jnp.zeros((D, EXTRA - 3 * WIDE), f32)], axis=1
    ).astype(bf16)
    lane = lax.broadcasted_iota(jnp.int32, (2, D), 1)
    edge = zed * WIDE
    inside = (lane >= edge) & (lane < edge + WIDE)
    own = jnp.concatenate(
        [
            jnp.sum(query_cot.astype(f32), axis=0, keepdims=True),
            jnp.sum(value_cot.astype(f32), axis=0, keepdims=True),
        ],
        axis=0,
    )
    own = jnp.where(inside, jnp.concatenate([own] * 4, axis=1), 0.0)
    vec = jnp.concatenate(
        [first_sums[0:1], second_sums[0:1], first_sums[1:3], second_sums[1:3], up_sums[...]], axis=0
    )
    extra = jnp.concatenate([own, vec, jnp.zeros((118, D), f32)], axis=0)
    extra = jnp.transpose(extra).astype(bf16)
    for f in range(F):
        slot = core if f % 2 == 0 else 1 - core
        packed[slot, f // 2, :, :EXTRA] = grads[48 * f : 48 * f + 48]
        packed[slot, f // 2, :, EXTRA:] = extra[48 * f : 48 * f + 48]
    stores = begin(sems, 0, (packed.at[1], send), (packed.at[0], mine))
    finish(stores)


def head_grad(blocks, cots, sums):
    half = shape((8, 48, D), bf16)
    return call(
        head_grad_kernel,
        "head_grad",
        (half, half),
        [HB] * 5 + [VM] * 6,
        [pltpu.VMEM((NBLK, BLK, D), bf16), pltpu.VMEM((2, 8, 48, D), bf16), dma(8)],
        mib=56,
        flops=2 * 10**9,
        nbytes=4 * 10**6,
        out_specs=(HB, HB),
    )(*blocks, *cots, *sums)


def centred(hidden):
    centre = hidden - jnp.mean(hidden, axis=-1, keepdims=True)
    inverse = lax.rsqrt(jnp.mean(centre * centre, axis=-1, keepdims=True) + epsilon)
    return centre * inverse, inverse


def norm_back(scaled, hat, inverse):
    return inverse * (
        scaled
        - jnp.mean(scaled, axis=-1, keepdims=True)
        - hat * jnp.mean(scaled * hat, axis=-1, keepdims=True)
    )


def pack_heads_kernel(vectors, b_up, w_qkv, w_out, copies, heads, qkv, sems):
    zed = places()[1]
    loads = begin(sems, 0, (w_qkv, qkv), (w_out, heads.at[pl.ds(48, 48)]))
    bias = b_up[...].astype(f32)
    small = jnp.concatenate([vectors[...].astype(f32)] + [bias[:, 48 * e : 48 * e + 48] for e in range(4)], axis=0)
    small = jnp.concatenate([small, jnp.zeros((12, 80), f32)], axis=1)
    small = jnp.concatenate([small, jnp.zeros((116, 128), f32)], axis=0)
    heads[0:48, EXTRA:] = jnp.transpose(small)[:48].astype(bf16)
    heads[0:48, 3 * WIDE : EXTRA] = jnp.zeros((48, EXTRA - 3 * WIDE), bf16)
    finish(loads)
    for z in range(4):

        @pl.when(zed == z)
        def _(z=z):
            heads[0:48, : 3 * WIDE] = jnp.concatenate(
                [qkv[:, D * t + WIDE * z : D * t + WIDE * z + WIDE] for t in range(3)], axis=1
            )

    finish(begin(sems, 2, *((heads, copies.at[k]) for k in range(8))))


def pack_feed_kernel(w_up, w_down, feed, feed_own, up, sems):
    half = lax.rem(places()[1], 2)
    start = pl.multiple_of(96 * half, 32)
    loads = begin(
        sems,
        0,
        (w_up, up),
        (w_down.at[pl.ds(start, 96)], feed_own.at[pl.ds(0, 96)]),
    )
    loads[0].wait()
    for h in range(2):

        @pl.when(half == h)
        def _(h=h):
            for e in range(2):
                first = 96 * h + 48 * e
                feed_own[96 + 48 * e : 144 + 48 * e, :] = jnp.concatenate(
                    [up[:, 192 * f + first : 192 * f + first + 48] for f in range(F)], axis=1
                )

    finish(loads[1:])
    finish(begin(sems, 2, *((feed_own, feed.at[k]) for k in range(8))))


def first_kernel(mix0, mix1, mix2, mix3, w_mine, w_other, vectors, tokens, low, norm, hat, *scratch):
    weights, mixes, norm_own, hat_own, sems = scratch
    xh, zed, core = places()
    loads = begin(sems, 0, *((mix, mixes.at[k]) for k, mix in enumerate((mix0, mix1, mix2, mix3))))
    loads += begin(sems, 4, *head_rows(w_mine, w_other, weights, 48))
    total = tokens[...].astype(f32) + vectors[2:3]
    finish(loads)
    for k in range(4):
        total += nn(mixes[k], weights[pl.ds(2 * (zed ^ k), 2)].reshape(WIDE, D))
    first_hat, first_inv = centred(total)
    first_norm = first_hat * vectors[4:5] + vectors[5:6]
    low[...] = first_norm.astype(bf16)
    norm_own[...] = first_norm
    hat_own[:, :D] = first_hat
    hat_own[:, D:] = jnp.broadcast_to(first_inv, (BLK, 128))
    finish(begin(sems, 0, (norm_own, norm), (hat_own, hat)))


def load_feed(w_mine, w_other, weights, sems, order):
    core = places()[2]
    loads = {}
    for k in order:
        rows = pl.ds(48 * k, 48)
        loads[k] = begin(
            sems,
            2 * k,
            (w_mine.at[:, rows], weights.at[k, :, core]),
            (w_other.at[:, rows], weights.at[k, :, 1 - core]),
        )
    return loads


def feed_kernel(mine, other, w_mine, w_other, vectors, activ, slope, keep, send, weights, sems):
    loads = load_feed(w_mine, w_other, weights, sems, (2, 0, 3, 1))
    rows = jnp.concatenate([mine[...], other[...]], axis=0)
    b_up = jnp.where(lax.rem(places()[1], 2) == 0, vectors[8:10], vectors[10:12])
    total = None
    for e in range(2):
        finish(loads[2 + e])
        up = nn(rows, weights[2 + e].reshape(D, D)) + b_up[e : e + 1, :]
        erf = lax.erf(up * root_half)
        low = (0.5 * up * (1.0 + erf)).astype(bf16)
        activ[:, D * e : D * e + D] = low
        slope[:, D * e : D * e + D] = (
            0.5 * (1.0 + erf) + up * jnp.exp(-0.5 * up * up) * inv_root_tau
        ).astype(bf16)
        finish(loads[e])
        part = nn(low, weights[e].reshape(D, D))
        total = part if total is None else total + part
    keep[...] = total[:BLK]
    send[...] = total[BLK:].astype(bf16)


def second_kernel(norm, keep, came, vectors, out_grad, layer_out, cot, low, sums):
    second_sum = norm[...] + (keep[...] + came[...].astype(f32)) + vectors[3:4]
    second_hat, second_inv = centred(second_sum)
    layer_out[...] = (second_hat * vectors[6:7] + vectors[7:8]).astype(bf16)
    out_cot = out_grad[...].astype(f32)
    second_cot = norm_back(out_cot * vectors[6:7], second_hat, second_inv)
    cot[...] = second_cot
    down_cot = second_cot.astype(bf16)
    low[...] = down_cot
    sums[0:1] = jnp.sum(down_cot.astype(f32), axis=0, keepdims=True)
    sums[1:2] = jnp.sum(out_cot * second_hat, axis=0, keepdims=True)
    sums[2:3] = jnp.sum(out_cot, axis=0, keepdims=True)


def feed_back_kernel(mine, other, w_mine, w_other, slope, up_cot, keep, send, sums, weights, sems):
    loads = load_feed(w_mine, w_other, weights, sems, (0, 2, 1, 3))
    rows = jnp.concatenate([mine[...], other[...]], axis=0)
    total = None
    for e in range(2):
        finish(loads[e] + loads[2 + e])
        w_down = weights[e].reshape(D, D)
        w_up = weights[2 + e].reshape(D, D)
        low = (nt(rows, w_down) * slope[:, D * e : D * e + D].astype(f32)).astype(bf16)
        up_cot[:, D * e : D * e + D] = low
        sums[e : e + 1, :] = jnp.sum(low.astype(f32), axis=0, keepdims=True)
        part = nt(low, w_up)
        total = part if total is None else total + part
    keep[...] = total[:BLK]
    send[...] = total[BLK:].astype(bf16)


def feed_grad_kernel(mine, other, low_mine, low_other, activ, up_cot, keep, send, packed, sems):
    xh, zed, core = places()
    down_cot = jnp.concatenate([mine[...], other[...]], axis=0)
    first_low = jnp.concatenate([low_mine[...], low_other[...]], axis=0)
    for e in range(2):
        down = tn(activ[:, D * e : D * e + D], down_cot).astype(bf16)
        up = tn(first_low, up_cot[:, D * e : D * e + D]).astype(bf16)
        for f in range(F):
            slot = core if f % 2 == 0 else 1 - core
            packed[slot, f // 2, 48 * e : 48 * e + 48, :] = down[48 * f : 48 * f + 48]
            packed[slot, f // 2, 96 + 48 * e : 144 + 48 * e, :] = up[48 * f : 48 * f + 48]
    finish(begin(sems, 0, (packed.at[1], send), (packed.at[0], keep)))


def first_back_kernel(
    cot, keep, came, vectors, hat, w_mine, w_other, mix0, mix1, mix2, mix3,
    input_cot, grad_keep, grad_send, back0, back1, back2, back3, sums,
    weights, mixes, hats, total_own, back, packed, sems,
):
    xh, zed, core = places()
    load_hat = begin(sems, 0, (hat, hats))
    loads = begin(sems, 1, *head_rows(w_mine, w_other, weights, 48))
    late = begin(sems, 3, *((mix, mixes.at[k]) for k, mix in enumerate((mix0, mix1, mix2, mix3))))
    first_cot = cot[...] + (keep[...] + came[...].astype(f32))
    finish(load_hat)
    first_hat = hats[:, :D]
    total = norm_back(first_cot * vectors[4:5], first_hat, hats[:, D : D + 1])
    total_own[...] = total
    attend_cot = total.astype(bf16)
    finish(loads)
    stores = begin(sems, 7, (total_own, input_cot))
    for k, out in enumerate((back0, back1, back2, back3)):
        back[k] = nt(attend_cot, weights[pl.ds(2 * (zed ^ k), 2)].reshape(WIDE, D)).astype(bf16)
        stores += begin(sems, 8 + k, (back.at[k], out))
    finish(late)
    for k in range(4):
        grads = tn(mixes[k], attend_cot).astype(bf16)
        for j in range(4):
            slot = core if j % 2 == 0 else 1 - core
            packed[slot, 2 * (zed ^ k) + j // 2] = grads[48 * j : 48 * j + 48]
    stores += begin(sems, 12, (packed.at[1], grad_send), (packed.at[0], grad_keep))
    sums[0:1] = jnp.sum(attend_cot.astype(f32), axis=0, keepdims=True)
    sums[1:2] = jnp.sum(first_cot * first_hat, axis=0, keepdims=True)
    sums[2:3] = jnp.sum(first_cot, axis=0, keepdims=True)
    finish(stores)


def pair_kernel(head_keep, head_came, out_keep, out_came, pair):
    pair[:, 0:48, :] = (head_keep[...].astype(f32) + head_came[...].astype(f32)).astype(bf16)
    pair[:, 48:96, :] = (out_keep[...].astype(f32) + out_came[...].astype(f32)).astype(bf16)


def feed_sum_kernel(parts, keep, send, slots, sems):
    high = lax.div(places()[1], 2)
    for m in range(2):
        total = parts[0, 96 * m : 96 * m + 96, :].astype(f32)
        for k in range(1, 8):
            total += parts[k, 96 * m : 96 * m + 96, :].astype(f32)
        slots[high ^ m] = total.astype(bf16)
    finish(begin(sems, 0, (slots.at[0], keep), (slots.at[1], send)))


def last_sum_kernel(heads, keep, came, total):
    total[0:96, :] = (keep[...].astype(f32) + came[...].astype(f32)).astype(bf16)
    whole = heads[0].astype(f32)
    for k in range(1, 8):
        whole += heads[k].astype(f32)
    total[96:192, :] = whole.astype(bf16)


def merge_kernel(own, other, merged):
    merged[...] = (own[...].astype(f32) + other[...].astype(f32)).astype(bf16)


def unpack_kernel(one0, one1, one2, one3, qkv, out, up, down, vectors, bias, every):
    zed = places()[1]
    for k, one in enumerate((one0, one1, one2, one3)):
        every[zed ^ k] = one[...]
    ups = []
    for h in range(2):
        down[96 * h : 96 * h + 96, :] = every[h, 0:96, :].astype(f32)
        ups.append([every[2 + h, 48 * e : 48 * e + 48, :].astype(f32) for e in range(2)])
    up[...] = jnp.concatenate(
        [ups[h][e][:, 48 * f : 48 * f + 48] for f in range(F) for h in range(2) for e in range(2)], axis=1
    )
    total = every[0, 144:192, :].astype(f32)
    for z in range(1, 4):
        total += every[z, 144:192, :].astype(f32)
    out[...] = total
    heads = [every[z, 96:144, :].astype(f32) for z in range(4)]
    for t in range(3):
        qkv[:, D * t : D * t + D] = jnp.concatenate(
            [heads[z][:, WIDE * t : WIDE * t + WIDE] for z in range(4)], axis=1
        )
    both = [heads[h][:, EXTRA:] + heads[2 + h][:, EXTRA:] for h in range(2)]
    small = [jnp.transpose(jnp.concatenate([one, jnp.zeros((80, 128), f32)], axis=0)) for one in both]
    vectors[...] = (small[0] + small[1])[0:8, 0:48]
    bias[...] = jnp.concatenate([small[0][8:10], small[1][8:10]], axis=0)[:, 0:48]


CHIPS = [[i for i in range(F) if i % 2 == k] for k in range(2)]


def swap(x, axis, size, bit):
    return lax.ppermute(x, axis, [(i, i ^ bit) for i in range(size)])


def a2a(x, axis, groups=None):
    return lax.all_to_all(x, axis, 0, 0, tiled=True, axis_index_groups=groups)


def body(tokens, w_qkv, w_out, w_up, w_down, vectors, b_up, lengths, block_seq, out_grad):
    after = lax.optimization_barrier

    token_other = swap(tokens, "ctx", NBLK, 1)
    heads_out = call(
        pack_heads_kernel,
        "pack_heads",
        shape((8, 96, D), bf16),
        [VM, VM, HB, HB],
        [pltpu.VMEM((96, D), bf16), pltpu.VMEM((48, 3 * D), bf16), dma(10)],
        mib=56,
        flops=10**6,
        nbytes=2 * 10**6,
        out_specs=HB,
    )(vectors, b_up.reshape(1, 192), w_qkv, w_out)
    w_up, heads_out, token_other = after((w_up, heads_out, token_other))
    pair = jnp.stack([tokens, token_other])
    pairs = [swap(pair, "ctx", NBLK, 2 * k) for k in (1, 2, 3)]
    feed_out = call(
        pack_feed_kernel,
        "pack_feed",
        shape((8, 192, D), bf16),
        [HB] * 2,
        [pltpu.VMEM((192, D), bf16), pltpu.VMEM((48, FF), bf16), dma(10)],
        mib=56,
        flops=10**6,
        nbytes=4 * 10**6,
        out_specs=HB,
    )(w_up, w_down)
    w1_mine = a2a(heads_out, "fsdp", CHIPS)
    w1_mine, feed_out, *pairs = after((w1_mine, feed_out, *pairs))
    w2_mine = a2a(feed_out, "fsdp", CHIPS)
    w1_other = swap(w1_mine, "fsdp", F, 1)

    blocks = [tokens, token_other, *pairs]
    rows, *kept, mix0, mix1, mix2, mix3 = attend(lengths, block_seq, blocks, w1_mine, w1_other)
    mixes = [mix0] + [swap(mix, "ctx", NBLK, 2 * (k + 1)) for k, mix in enumerate((mix1, mix2, mix3))]
    first_low, first_norm, first_hat = call(
        first_kernel,
        "first",
        (shape((BLK, D), bf16), shape((BLK, D)), shape((BLK, D + 128))),
        [HB] * 6 + [VM, VM],
        [
            pltpu.VMEM((8, 2, 48, D), bf16),
            pltpu.VMEM((4, BLK, WIDE), bf16),
            pltpu.VMEM((BLK, D), f32),
            pltpu.VMEM((BLK, D + 128), f32),
            dma(6),
        ],
        mib=56,
        flops=2 * BLK * D * D,
        nbytes=4 * 10**6,
        out_specs=(VM, HB, HB),
    )(*mixes, w1_mine, w1_other, rows, tokens)
    low_other = swap(first_low, "ctx", NBLK, 2)
    w2_mine, first_norm = after((w2_mine, first_norm))
    w2_other = swap(w2_mine, "fsdp", F, 1)
    loaded = [pltpu.VMEM((4, 8, 2, 48, D), bf16), dma(8)]
    activ, slope, keep, send = call(
        feed_kernel,
        "feed",
        (shape((2 * BLK, HALF), bf16), shape((2 * BLK, HALF), bf16), shape((BLK, D)), shape((BLK, D), bf16)),
        [VM, VM, HB, HB, VM],
        loaded,
        flops=8 * BLK * D * HALF,
        nbytes=8 * 10**6,
    )(first_low, low_other, w2_mine, w2_other, rows)
    came = swap(send, "ctx", NBLK, 2)
    layer_out, second_cot, down_cot, second_sums = call(
        second_kernel,
        "second",
        (shape((BLK, D), bf16), shape((BLK, D)), shape((BLK, D), bf16), shape((3, D))),
        [VM] * 5,
        flops=10**7,
        nbytes=2 * 10**6,
    )(first_norm, keep, came, rows, out_grad)
    down_other = swap(down_cot, "ctx", NBLK, 2)
    up_cot, keep, send, up_sums = call(
        feed_back_kernel,
        "feed_back",
        (shape((2 * BLK, HALF), bf16), shape((BLK, D)), shape((BLK, D), bf16), shape((2, D))),
        [VM, VM, HB, HB, VM],
        loaded,
        flops=8 * BLK * D * HALF,
        nbytes=8 * 10**6,
    )(down_cot, down_other, w2_mine, w2_other, slope)
    came = swap(send, "ctx", NBLK, 2)
    feed_part = shape((8, 192, D), bf16)
    feed_keep, feed_send = call(
        feed_grad_kernel,
        "feed_grad",
        (feed_part, feed_part),
        [VM] * 6,
        [pltpu.VMEM((2, 8, 192, D), bf16), dma(2)],
        mib=20,
        flops=8 * BLK * D * HALF,
        nbytes=8 * 10**6,
        out_specs=(HB, HB),
    )(down_cot, down_other, first_low, low_other, activ, up_cot)
    feed_send, came = after((feed_send, came))
    feed_came = swap(feed_send, "fsdp", F, 1)
    out_part = shape((8, 48, D), bf16)
    back_part = shape((BLK, WIDE), bf16)
    input_cot, out_keep, out_send, back0, back1, back2, back3, first_sums = call(
        first_back_kernel,
        "first_back",
        (shape((BLK, D)), out_part, out_part, back_part, back_part, back_part, back_part, shape((3, D))),
        [VM] * 4 + [HB] * 7,
        [
            pltpu.VMEM((8, 2, 48, D), bf16),
            pltpu.VMEM((4, BLK, WIDE), bf16),
            pltpu.VMEM((BLK, D + 128), f32),
            pltpu.VMEM((BLK, D), f32),
            pltpu.VMEM((4, BLK, WIDE), bf16),
            pltpu.VMEM((2, 8, 48, D), bf16),
            dma(14),
        ],
        flops=4 * BLK * D * D,
        nbytes=4 * 10**6,
        out_specs=(HB,) * 7 + (VM,),
    )(second_cot, keep, came, rows, first_hat, w1_mine, w1_other, *mixes)
    def add(one, two):
        return (one.astype(f32) + two.astype(f32)).astype(bf16)

    feed_pair, back1, back2, back3 = after((add(feed_keep, feed_came), back1, back2, back3))
    feed_parts = a2a(feed_pair, "fsdp", CHIPS)
    cots = [back0] + [swap(back, "ctx", NBLK, 2 * (k + 1)) for k, back in enumerate((back1, back2, back3))]
    out_came = swap(out_send, "fsdp", F, 1)

    *head_cots, part0, part1, part2, part3 = attend_back(block_seq, w1_mine, w1_other, cots, kept)
    partials = (part0, part1, part2, part3)
    head_keep, head_send = head_grad(blocks, head_cots, (first_sums, second_sums, up_sums))
    head_came = swap(head_send, "fsdp", F, 1)
    token_parts = [swap(partials[k], "ctx", NBLK, 2 * k) for k in (1, 2, 3)]
    pair = call(pair_kernel, "pair", shape((8, 96, D), bf16), [VM] * 4, flops=10**6, nbytes=4 * 10**6)(
        head_keep, head_came, out_keep, out_came
    )
    head_parts = a2a(pair, "fsdp", CHIPS)

    ffn = shape((96, D), bf16)
    feed_rows, feed_sent = call(
        feed_sum_kernel,
        "feed_sum",
        (ffn, ffn),
        [VM],
        [pltpu.VMEM((2, 96, D), bf16), dma(2)],
        mib=56,
        flops=10**6,
        nbytes=3 * 10**6,
        out_specs=(HB, HB),
    )(feed_parts)
    parts = [feed_rows, swap(feed_sent, "ctx", NBLK, 4)]
    head_parts, token_parts, parts = after((head_parts, token_parts, parts))
    total = call(last_sum_kernel, "last_sum", shape((192, D), bf16), [VM] * 3, flops=10**6, nbytes=2 * 10**6)(
        head_parts, *parts
    )
    merged = call(merge_kernel, "merge", shape((192, D), bf16), [VM] * 2, flops=10**6, nbytes=10**6)(
        total, swap(total, "ctx", NBLK, 1)
    )
    every = [merged] + [swap(merged, "ctx", NBLK, 2 * k) for k in (1, 2, 3)]
    by_z = partials[0].astype(f32)
    for part in token_parts:
        by_z += part.astype(f32)
    by_z = by_z.astype(bf16)
    tokens_grad = input_cot + by_z[0].astype(f32) + swap(by_z[1], "ctx", NBLK, 1).astype(f32)
    qkv_grad, out_grad_w, up_grad, down_grad, vectors_grad, bias_grad = call(
        unpack_kernel,
        "unpack",
        (shape((48, 3 * D)), shape((48, D)), shape((48, FF)), shape((192, D)), shape((8, 48)), shape((4, 48))),
        [VM] * 4,
        [pltpu.VMEM((4, 192, D), bf16)],
        flops=10**6,
        nbytes=4 * 10**6,
    )(*every)
    return (layer_out, tokens_grad, qkv_grad, out_grad_w, up_grad, down_grad, vectors_grad, bias_grad.reshape(192))


def solution(mesh):
    by_token = P(("fsdp", "ctx"), None)
    by_row = P("fsdp", None)
    in_specs = (
        by_token, by_row, by_row, by_row, by_row, P(None, "fsdp"), P("fsdp"), by_row, by_row, by_token,
    )
    out_specs = (by_token, by_token, by_row, by_row, by_row, by_row, P(None, "fsdp"), P("fsdp"))
    return jax.shard_map(body, mesh=mesh, in_specs=in_specs, out_specs=out_specs, check_vma=False)
```
